512 devices in a mesh: section: 4 (over z_hi, core), ctx: 128 (over z_lo, x, y).
Axes of the slice: x: 4, y: 4, z: 16 (z_hi: 2, z_lo: 8; z = z_hi * 8 + z_lo), core: 2. Of those that a mesh axis runs over, the one named last changes fastest.
Arguments:
- query: bfloat16 [4, 2048, 6144], P('section', 'ctx'), may hold values from -96 to 96
- key: bfloat16 [4, 2048, 1024], P('section', 'ctx'), may hold values from -9.6 to 9.6
- value: bfloat16 [4, 2048, 1024], P('section', 'ctx'), may hold values from -6 to 6
- clean_key: bfloat16 [4, 2048, 1024], P('section', 'ctx'), may hold values from -9.5625 to 9.5625
- clean_value: bfloat16 [4, 2048, 1024], P('section', 'ctx'), may hold values from -6 to 6
- completing: int32 [1], replicated, may hold values from 0 to 2
- span_mask: int32 [4, 4], replicated, may hold values from 0 to 1, as said below
Outputs:
- attended: bfloat16 [4, 2048, 6144], P('section', 'ctx')
The draws below stay inside these ranges and needn't reach their ends.
Inputs may be any that keep to these rules, and one draw needn't show every extreme that they name: span_mask is 1 on the diagonal and just below it, 0 above it, and 0 or 1 elsewhere below it.
All inputs are finite; a program needn't handle non-finite values.
Results may differ from the reference program's by a relative error of at most 0.0045.
Values may be sent and summed in bfloat16 or wider, within the bound.
No kernel may reach another device: no remote copies, remote signals or barrier semaphores. Data moves between devices by JAX's collectives and lax.ppermute only.
A program may use at most 64 MiB of HBM per device.

```python
import math
import jax
import jax.numpy as jnp
from jax import lax

HEAD_DIM = 128
HEADS = 48
KV_HEADS = 8
SECTIONS = 4
SPAN = 2048


def shared_keys(key):
    base = jax.random.normal(jax.random.fold_in(key, 101), (SECTIONS, SPAN, KV_HEADS, HEAD_DIM), jnp.float32)
    return 1.6 * jnp.clip(base, -6.0, 6.0)


def draw_query(key, part):
    key = jax.random.fold_in(key, 3)
    group = HEADS // KV_HEADS
    own = 1.6 * jnp.clip(jax.random.normal(key, (SECTIONS, SPAN, KV_HEADS, group, HEAD_DIM), jnp.float32), -6.0, 6.0)
    return own.reshape(SECTIONS, SPAN, HEADS * HEAD_DIM).astype(jnp.bfloat16)


def draw_key(key, part):
    common = shared_keys(key)
    return common.reshape(SECTIONS, SPAN, KV_HEADS * HEAD_DIM).astype(jnp.bfloat16)


def draw_span_mask(key, part):
    key = jax.random.fold_in(key, 9)
    coins = jax.random.randint(key, (SECTIONS, SECTIONS), 0, 2)
    rows = jnp.arange(SECTIONS)[:, None]
    cols = jnp.arange(SECTIONS)[None, :]
    near = jnp.logical_and(cols >= rows - 1, cols <= rows)
    return jnp.where(near, 1, jnp.where(cols > rows, 0, coins)).astype(jnp.int32)


def shard_levels(rng, shape, shards, smallest, top_value):
    factor_of = 1.0
    for dim, parts in shards:
        heights = jax.random.uniform(jax.random.fold_in(jax.random.fold_in(rng, 6), dim), (parts,), jnp.float32, smallest / len(shards), top_value / len(shards))
        factor_of = factor_of * jnp.repeat(jnp.exp(heights), shape[dim] // parts).reshape((-1,) + (1,) * (len(shape) - 1 - dim))
    return factor_of


def bell_draw(stream_key, dims, width, limit, split=(), kind=jnp.bfloat16):
    drawn = jax.random.normal(stream_key, dims, jnp.float32) * width
    if len(split) > 0:
        drawn = shard_levels(stream_key, dims, split, -0.22, 0.18) * drawn
    return jnp.clip(drawn, min=-limit, max=limit).astype(kind)


def setup_inputs(seed: int = 0) -> dict:
    splits = jax.random.split(jax.random.key(seed), 8)
    query = draw_query(jax.random.fold_in(splits[7], 71), 0)
    key = draw_key(jax.random.fold_in(splits[7], 71), 0)
    value = bell_draw(splits[2], (SECTIONS, SPAN, KV_HEADS * HEAD_DIM), 1.0, 6.0, ((0, 4), (1, 128)))
    clean_key = bell_draw(splits[3], (SECTIONS, SPAN, KV_HEADS * HEAD_DIM), 1.6, 9.5625, ((0, 4), (1, 128)))
    clean_value = bell_draw(splits[4], (SECTIONS, SPAN, KV_HEADS * HEAD_DIM), 1.0, 6.0, ((0, 4), (1, 128)))
    completing = jax.random.randint(splits[5], (1,), 0, SECTIONS - 1).astype(jnp.int32)
    span_mask = draw_span_mask(jax.random.fold_in(splits[7], 71), 0)
    return dict(query=query, key=key, value=value, clean_key=clean_key, clean_value=clean_value, completing=completing, span_mask=span_mask)


def attend_block(query_rows, keys_all, values_all, valid):
    scale = HEAD_DIM ** -0.5
    scores = jnp.einsum("bkgd,nkd->kgbn", query_rows.astype(jnp.float32), keys_all.astype(jnp.float32)) * scale
    scores = jnp.where(valid[None, None, None, :], scores, -1e30)
    top = jnp.max(scores, axis=-1, keepdims=True)
    weights = jnp.exp(scores - top)
    total = jnp.sum(weights, axis=-1)
    weights_b = lax.optimization_barrier(weights.astype(jnp.bfloat16)).astype(jnp.float32)
    summed = jnp.einsum("kgbn,nkd->bkgd", weights_b, values_all.astype(jnp.float32))
    result = summed / jnp.transpose(total, (2, 0, 1))[..., None]
    return result.astype(jnp.bfloat16).reshape(query_rows.shape[0], HEADS * HEAD_DIM)


def reference(query, key, value, clean_key, clean_value, completing, span_mask):
    group = HEADS // KV_HEADS
    block_rows = math.gcd(SPAN, 128)
    finished = completing[0]
    handed_keys = lax.dynamic_index_in_dim(clean_key, finished, 0, keepdims=False)
    handed_values = lax.dynamic_index_in_dim(clean_value, finished, 0, keepdims=False)
    outputs = []
    for section_now in range(SECTIONS):
        seen = jnp.logical_and(section_now > finished, span_mask[section_now, finished] == 1)
        keys_all = jnp.concatenate([key[section_now], handed_keys], axis=0).reshape(2 * SPAN, KV_HEADS, HEAD_DIM)
        values_all = jnp.concatenate([value[section_now], handed_values], axis=0).reshape(2 * SPAN, KV_HEADS, HEAD_DIM)
        valid = jnp.concatenate([jnp.ones((SPAN,), bool), jnp.broadcast_to(seen, (SPAN,))])
        blocks = query[section_now].reshape(SPAN // block_rows, block_rows, KV_HEADS, group, HEAD_DIM)
        result = lax.map(lambda rows: attend_block(rows, keys_all, values_all, valid), blocks)
        outputs.append(result.reshape(SPAN, HEADS * HEAD_DIM))
    return jnp.stack(outputs)
```

```python
import functools
import math

import jax
import jax.numpy as jnp
from jax import lax
from jax.experimental import pallas as pl
from jax.experimental.pallas import tpu as pltpu
from jax.sharding import Mesh
from jax.sharding import PartitionSpec as P

HEAD_DIM = 128
HEADS = 48
KV_HEADS = 8
GROUP = HEADS // KV_HEADS
WIDE = GROUP * HEAD_DIM
BASE = HEAD_DIM**-0.5 * math.log2(math.e)
VMEM = pl.BlockSpec(memory_space=pltpu.VMEM)
SMEM = pl.BlockSpec(memory_space=pltpu.SMEM)


def head_rows(q_ref, first, count):
    rows = q_ref.shape[0] * q_ref.shape[1]
    return jnp.concatenate(
        [
            q_ref[:, :, g * HEAD_DIM : (g + 1) * HEAD_DIM].reshape(rows, HEAD_DIM)
            for g in range(first, first + count)
        ],
        0,
    )


def attend(q, k, v_ones):
    scores = lax.dot_general(q, k, (((1,), (1,)), ((), ())), preferred_element_type=jnp.float32)
    largest = jnp.max(scores, axis=-1, keepdims=True)
    weights = jnp.exp2((scores - largest) * BASE).astype(jnp.bfloat16)
    return largest, jnp.dot(weights, v_ones, preferred_element_type=jnp.float32)


def with_ones(v):
    return jnp.concatenate([v, jnp.ones_like(v)], 1)


def own_kernel(count, q_ref, kv_ref, sums_ref, largest_ref):
    n = kv_ref.shape[0] * kv_ref.shape[1]
    rows = q_ref.shape[0] * q_ref.shape[1]
    k = kv_ref[:, :, :HEAD_DIM].reshape(n, HEAD_DIM)
    v_ones = with_ones(kv_ref[:, :, HEAD_DIM : 2 * HEAD_DIM].reshape(n, HEAD_DIM))
    for first in range(0, GROUP, count):
        at = slice(first * rows, (first + count) * rows)
        largest, sums = attend(head_rows(q_ref, first, count), k, v_ones)
        sums_ref[at, :] = sums
        largest_ref[at, :] = jnp.broadcast_to(largest, (count * rows, HEAD_DIM))


def far_kernel(count, flags_ref, q_ref, kv_ref, other_ref, sums_ref, largest_ref, out_ref):
    n = kv_ref.shape[0] * kv_ref.shape[1]
    blocks, rows_each = q_ref.shape[0], q_ref.shape[1]
    rows = blocks * rows_each

    def store(first, total):
        out = total[:, :HEAD_DIM] / total[:, HEAD_DIM:]
        for i in range(count):
            g = first + i
            out_ref[:, :, g * HEAD_DIM : (g + 1) * HEAD_DIM] = (
                out[i * rows : (i + 1) * rows].astype(out_ref.dtype).reshape(blocks, rows_each, HEAD_DIM)
            )

    @pl.when(flags_ref[0] == 1)
    def _():
        mine = kv_ref[:, :, 2 * HEAD_DIM :].reshape(n, HEAD_DIM)
        other = other_ref[...].reshape(n, HEAD_DIM)
        keys_here = flags_ref[1] == 0
        k = jnp.where(keys_here, mine, other)
        v_ones = with_ones(jnp.where(keys_here, other, mine))
        for first in range(0, GROUP, count):
            at = slice(first * rows, (first + count) * rows)
            largest, sums = attend(head_rows(q_ref, first, count), k, v_ones)
            before = largest_ref[at, :]
            after = jnp.maximum(before, largest)
            old = jnp.exp2((before - after) * BASE)
            new = jnp.exp2((largest - after) * BASE)
            old, new = jnp.concatenate([old, old], 1), jnp.concatenate([new, new], 1)
            store(first, sums_ref[at, :] * old + sums * new)

    @pl.when(flags_ref[0] == 0)
    def _():
        for first in range(0, GROUP, count):
            store(first, sums_ref[first * rows : (first + count) * rows, :])


def estimate(q_rows, n):
    return pl.CostEstimate(flops=4 * q_rows * n * HEAD_DIM, bytes_accessed=4 * 2**20, transcendentals=q_rows * n)


def own_attention(q, kv):
    rows, n = q.shape[0] * q.shape[1] * GROUP, kv.shape[0] * kv.shape[1]
    return pl.pallas_call(
        functools.partial(own_kernel, 3),
        out_shape=(
            jax.ShapeDtypeStruct((rows, 2 * HEAD_DIM), jnp.float32),
            jax.ShapeDtypeStruct((rows, HEAD_DIM), jnp.float32),
        ),
        in_specs=[VMEM] * 2,
        out_specs=(VMEM,) * 2,
        cost_estimate=estimate(rows, n),
        compiler_params=pltpu.CompilerParams(vmem_limit_bytes=40 * 2**20),
    )(q, kv)


def far_attention(flags, q, kv, other, sums, largest):
    rows, n = q.shape[0] * q.shape[1] * GROUP, kv.shape[0] * kv.shape[1]
    return pl.pallas_call(
        functools.partial(far_kernel, 3),
        out_shape=jax.ShapeDtypeStruct((q.shape[0], q.shape[1], WIDE), jnp.bfloat16),
        in_specs=[SMEM] + [VMEM] * 5,
        out_specs=VMEM,
        cost_estimate=estimate(rows, n),
        compiler_params=pltpu.CompilerParams(vmem_limit_bytes=40 * 2**20),
    )(flags, q, kv, other, sums, largest)


def shards(query, key, value, clean_key, clean_value, completing, span_mask):
    tok = query.shape[1]
    section = lax.axis_index("section")
    core, half = section % 2, section // 2
    finished = completing[0]
    seen = jnp.logical_and(section > finished, span_mask[section, finished] == 1)

    mine = jnp.where(core == 0, clean_key[0], clean_value[0])
    sent = jnp.where(core == 0, clean_value[0], clean_key[0])
    swapped = lax.ppermute(sent, "section", [(0, 1), (1, 0), (2, 3), (3, 2)])
    picked = jnp.where(finished % 2 == core, mine, swapped)
    handed = lax.ppermute(picked, "section", [(0, 2), (1, 3)])
    picked = jnp.where(jnp.logical_and(half == 1, finished < 2), handed, picked)

    def split(a):
        return a.reshape(tok, KV_HEADS, -1)

    packed = jnp.concatenate([split(query), split(key), split(value), split(picked)], -1)
    packed = jnp.transpose(packed, (1, 0, 2))
    served = lax.all_to_all(packed, "z", 0, 0, tiled=True)
    kv = served[:, :, WIDE:].reshape(1, KV_HEADS * tok, 3 * HEAD_DIM)
    plane = lax.axis_size("x") * lax.axis_size("y")
    kv = lax.all_to_all(jnp.broadcast_to(kv, (plane,) + kv.shape[1:]), ("x", "y"), 0, 0, tiled=True)
    other = lax.ppermute(kv[:, :, 2 * HEAD_DIM :], "section", [(0, 1), (1, 0), (2, 3), (3, 2)])
    sums, largest = own_attention(served, kv)
    flags = jnp.stack([seen.astype(jnp.int32), core.astype(jnp.int32)])
    out = far_attention(flags, served, kv, other, sums, largest)
    out = lax.all_to_all(out, "z", 0, 0, tiled=True)
    return jnp.transpose(out, (1, 0, 2)).reshape(1, tok, HEADS * HEAD_DIM)


def solution(mesh):
    grid = Mesh(mesh.devices.reshape(4, 8, 4, 4), ("section", "z", "x", "y"))
    rows = P("section", ("z", "x", "y"), None)
    return jax.shard_map(
        shards, mesh=grid, in_specs=(rows,) * 5 + (P(), P()), out_specs=rows, check_vma=False
    )
```

```python
import functools
import math

import jax
import jax.numpy as jnp
from jax import lax
from jax.experimental import pallas as pl
from jax.experimental.pallas import tpu as pltpu
from jax.sharding import Mesh
from jax.sharding import PartitionSpec as P

HEAD_DIM = 128
HEADS = 48
KV_HEADS = 8
GROUP = HEADS // KV_HEADS
WIDE = GROUP * HEAD_DIM
BASE = HEAD_DIM**-0.5 * math.log2(math.e)
VMEM = pl.BlockSpec(memory_space=pltpu.VMEM)
SMEM = pl.BlockSpec(memory_space=pltpu.SMEM)


def head_rows(q_ref, first, count):
    rows = q_ref.shape[0] * q_ref.shape[1]
    return jnp.concatenate(
        [
            q_ref[:, :, g * HEAD_DIM : (g + 1) * HEAD_DIM].reshape(rows, HEAD_DIM)
            for g in range(first, first + count)
        ],
        0,
    )


def attend(q, k, v_ones):
    scores = lax.dot_general(q, k, (((1,), (1,)), ((), ())), preferred_element_type=jnp.float32)
    largest = jnp.max(scores, axis=-1, keepdims=True)
    weights = jnp.exp2((scores - largest) * BASE).astype(jnp.bfloat16)
    return largest, jnp.dot(weights, v_ones, preferred_element_type=jnp.float32)


def with_ones(v):
    return jnp.concatenate([v, jnp.ones_like(v)], 1)


def own_kernel(count, q_ref, kv_ref, sums_ref, largest_ref):
    n = kv_ref.shape[0] * kv_ref.shape[1]
    rows = q_ref.shape[0] * q_ref.shape[1]
    k = kv_ref[:, :, :HEAD_DIM].reshape(n, HEAD_DIM)
    v_ones = with_ones(kv_ref[:, :, HEAD_DIM : 2 * HEAD_DIM].reshape(n, HEAD_DIM))
    for first in range(0, GROUP, count):
        at = slice(first * rows, (first + count) * rows)
        largest, sums = attend(head_rows(q_ref, first, count), k, v_ones)
        sums_ref[at, :] = sums
        largest_ref[at, :] = jnp.broadcast_to(largest, (count * rows, HEAD_DIM))


def far_kernel(count, completing_ref, mask_ref, q_ref, kv_ref, other_ref, sums_ref, largest_ref, out_ref):
    n = kv_ref.shape[0] * kv_ref.shape[1]
    blocks, rows_each = q_ref.shape[0], q_ref.shape[1]
    rows = blocks * rows_each
    core = lax.axis_index("core")
    section = lax.axis_index("half") * 2 + core
    finished = completing_ref[0]
    seen = jnp.logical_and(section > finished, mask_ref[section, finished] == 1)

    def store(first, total):
        out = total[:, :HEAD_DIM] / total[:, HEAD_DIM:]
        for i in range(count):
            g = first + i
            out_ref[:, :, g * HEAD_DIM : (g + 1) * HEAD_DIM] = (
                out[i * rows : (i + 1) * rows].astype(out_ref.dtype).reshape(blocks, rows_each, HEAD_DIM)
            )

    @pl.when(seen)
    def _():
        mine = kv_ref[:, :, 2 * HEAD_DIM :].reshape(n, HEAD_DIM)
        other = other_ref[...].reshape(n, HEAD_DIM)
        keys_here = core == 0
        k = jnp.where(keys_here, mine, other)
        v_ones = with_ones(jnp.where(keys_here, other, mine))
        for first in range(0, GROUP, count):
            at = slice(first * rows, (first + count) * rows)
            largest, sums = attend(head_rows(q_ref, first, count), k, v_ones)
            before = largest_ref[at, :]
            after = jnp.maximum(before, largest)
            old = jnp.exp2((before - after) * BASE)
            new = jnp.exp2((largest - after) * BASE)
            old, new = jnp.concatenate([old, old], 1), jnp.concatenate([new, new], 1)
            store(first, sums_ref[at, :] * old + sums * new)

    @pl.when(jnp.logical_not(seen))
    def _():
        for first in range(0, GROUP, count):
            store(first, sums_ref[first * rows : (first + count) * rows, :])


def stage_kernel(
    query_ref, key_ref, value_ref, clean_key_ref, clean_value_ref, out_ref, near_ref, mine_ref, sent_ref, sems
):
    core = lax.axis_index("core")
    copies = [
        pltpu.make_async_copy(query_ref.at[0, :, pl.ds(h * WIDE, WIDE)], out_ref.at[h], sems.at[h])
        for h in range(KV_HEADS)
    ]
    copies.append(pltpu.make_async_copy(key_ref.at[0], near_ref.at[0], sems.at[KV_HEADS]))
    copies.append(pltpu.make_async_copy(value_ref.at[0], near_ref.at[1], sems.at[KV_HEADS + 1]))
    for here, kept, given in ((0, clean_key_ref, clean_value_ref), (1, clean_value_ref, clean_key_ref)):

        @pl.when(core == here)
        def _():
            pltpu.make_async_copy(given.at[0], sent_ref, sems.at[KV_HEADS + 2]).start()
            pltpu.make_async_copy(kept.at[0], mine_ref, sems.at[KV_HEADS + 3]).start()

    for copy in copies:
        copy.start()
    for copy in copies:
        copy.wait()
    pltpu.make_async_copy(clean_key_ref.at[0], sent_ref, sems.at[KV_HEADS + 2]).wait()
    pltpu.make_async_copy(clean_key_ref.at[0], mine_ref, sems.at[KV_HEADS + 3]).wait()


def pack_keys_kernel(completing_ref, near_ref, picked_ref, handed_ref, after_ref, out_ref):
    del after_ref
    handed = jnp.logical_and(lax.axis_index("half") == 1, completing_ref[0] < 2)
    clean = jnp.where(handed, handed_ref[...], picked_ref[...])
    for h in range(KV_HEADS):
        at = slice(h * HEAD_DIM, (h + 1) * HEAD_DIM)
        first = (h % 2) * 3 * HEAD_DIM
        for z in (h // 2, h // 2 + KV_HEADS // 2):
            for i, part in enumerate((near_ref[0, :, at], near_ref[1, :, at], clean[:, at])):
                out_ref[z, :, first + i * HEAD_DIM : first + (i + 1) * HEAD_DIM] = part


def spread_kernel(served_ref, out_ref):
    rows = served_ref.shape[0] * served_ref.shape[1]
    each = 3 * HEAD_DIM
    for i in range(out_ref.shape[0]):
        head = (i // 4) % 2
        out_ref[i] = served_ref[:, :, head * each : (head + 1) * each].reshape(rows, each)


def estimate(q_rows, n):
    return pl.CostEstimate(flops=4 * q_rows * n * HEAD_DIM, bytes_accessed=4 * 2**20, transcendentals=q_rows * n)


def call(kernel, out_shape, specs, *operands, cost=None):
    outs = (VMEM,) * len(out_shape) if isinstance(out_shape, tuple) else VMEM
    return pl.pallas_call(
        kernel,
        out_shape=out_shape,
        in_specs=specs,
        out_specs=outs,
        cost_estimate=cost,
        compiler_params=pltpu.CompilerParams(vmem_limit_bytes=40 * 2**20),
    )(*operands)


def shaped(*shape, dtype=jnp.bfloat16):
    return jax.ShapeDtypeStruct(shape, dtype)


def shards(query, key, value, clean_key, clean_value, completing, span_mask):
    tok = query.shape[1]
    heads = KV_HEADS
    z_all, served_by, plane_axes = ("zq", "zc"), ("zc", "xb"), ("xa", "xb", "y")
    depth, plane = 8, 16
    anywhere = pl.BlockSpec(memory_space=pl.ANY)

    width = heads * HEAD_DIM
    packed, near, mine, sent = pl.pallas_call(
        stage_kernel,
        out_shape=(shaped(heads, tok, WIDE), shaped(2, tok, width), shaped(tok, width), shaped(tok, width)),
        in_specs=[anywhere] * 5,
        out_specs=(VMEM,) * 4,
        scratch_shapes=[pltpu.SemaphoreType.DMA((heads + 4,))],
    )(query, key, value, clean_key, clean_value)
    served = lax.all_to_all(packed, served_by, 0, 0, tiled=True)

    swapped = lax.ppermute(sent, "core", [(0, 1), (1, 0)])
    picked = jnp.where(completing[0] % 2 == lax.axis_index("core"), mine, swapped)
    handed = lax.ppermute(
        picked, ("half",) + z_all, [(z, depth + (z + depth // 2) % depth) for z in range(depth)]
    )

    kv = call(
        pack_keys_kernel,
        shaped(depth, tok, 6 * HEAD_DIM),
        [SMEM] + [VMEM] * 3 + [anywhere],
        completing,
        near,
        picked,
        handed,
        served,
    )
    kv = lax.all_to_all(kv, z_all, 0, 0, tiled=True)
    kv = call(spread_kernel, shaped(plane, depth * tok, 3 * HEAD_DIM), [VMEM], kv)
    kv = lax.all_to_all(kv, plane_axes, 0, 0, tiled=True)
    other = lax.ppermute(kv[:, :, 2 * HEAD_DIM :], "core", [(0, 1), (1, 0)])

    rows, n = heads * tok * GROUP, plane * depth * tok
    sums, largest = call(
        functools.partial(own_kernel, 3),
        (shaped(rows, 2 * HEAD_DIM, dtype=jnp.float32), shaped(rows, HEAD_DIM, dtype=jnp.float32)),
        [VMEM] * 2,
        served,
        kv,
        cost=estimate(rows, n),
    )
    out = call(
        functools.partial(far_kernel, 3),
        shaped(heads, tok, WIDE),
        [SMEM] * 2 + [VMEM] * 5,
        completing,
        span_mask,
        served,
        kv,
        other,
        sums,
        largest,
        cost=estimate(rows, n),
    )
    out = lax.all_to_all(out, served_by, 0, 0, tiled=True)
    return jnp.transpose(out, (1, 0, 2)).reshape(1, tok, HEADS * HEAD_DIM)


def solution(mesh):
    grid = Mesh(mesh.devices.reshape(2, 2, 2, 4, 2, 2, 4), ("half", "core", "zq", "zc", "xa", "xb", "y"))
    rows = P(("half", "core"), ("zq", "zc", "xa", "xb", "y"), None)
    return jax.shard_map(
        shards, mesh=grid, in_specs=(rows,) * 5 + (P(), P()), out_specs=rows, check_vma=False
    )
```

```python
import functools
import math

import jax
import jax.numpy as jnp
from jax import lax
from jax.experimental import pallas as pl
from jax.experimental.pallas import tpu as pltpu
from jax.sharding import Mesh
from jax.sharding import PartitionSpec as P

HEAD_DIM = 128
HEADS = 48
KV_HEADS = 8
GROUP = HEADS // KV_HEADS
WIDE = GROUP * HEAD_DIM
BASE = HEAD_DIM**-0.5 * math.log2(math.e)
VMEM = pl.BlockSpec(memory_space=pltpu.VMEM)
SMEM = pl.BlockSpec(memory_space=pltpu.SMEM)


def head_rows(q_ref, first, count):
    rows = q_ref.shape[0] * q_ref.shape[1]
    return jnp.concatenate(
        [
            q_ref[:, :, g * HEAD_DIM : (g + 1) * HEAD_DIM].reshape(rows, HEAD_DIM)
            for g in range(first, first + count)
        ],
        0,
    )


def scores_of(q, k):
    return lax.dot_general(q, k, (((1,), (1,)), ((), ())), preferred_element_type=jnp.float32)


def weigh(scores, v_ones):
    largest = jnp.max(scores, axis=-1, keepdims=True)
    weights = jnp.exp2((scores - largest) * BASE).astype(jnp.bfloat16)
    return largest, jnp.dot(weights, v_ones, preferred_element_type=jnp.float32)


def with_ones(v):
    return jnp.concatenate([v, jnp.ones_like(v)], 1)


def own_kernel(count, q_ref, kv_ref, sums_ref, largest_ref):
    n = kv_ref.shape[0] * kv_ref.shape[1]
    rows = q_ref.shape[0] * q_ref.shape[1]
    k = kv_ref[:, :, :HEAD_DIM].reshape(n, HEAD_DIM)
    v_ones = with_ones(kv_ref[:, :, HEAD_DIM : 2 * HEAD_DIM].reshape(n, HEAD_DIM))
    firsts = range(0, GROUP, count)
    scores = [scores_of(head_rows(q_ref, first, count), k) for first in firsts]
    for first, block in zip(firsts, scores):
        at = slice(first * rows, (first + count) * rows)
        largest, sums = weigh(block, v_ones)
        sums_ref[at, :] = sums
        largest_ref[at, :] = jnp.broadcast_to(largest, (count * rows, HEAD_DIM))


def far_kernel(count, completing_ref, mask_ref, q_ref, kv_ref, other_ref, sums_ref, largest_ref, out_ref):
    n = kv_ref.shape[0] * kv_ref.shape[1]
    blocks, rows_each = q_ref.shape[0], q_ref.shape[1]
    rows = blocks * rows_each
    core = lax.axis_index("core")
    section = lax.axis_index("half") * 2 + core
    finished = completing_ref[0]
    seen = jnp.logical_and(section > finished, mask_ref[section, finished] == 1)

    def store(first, total):
        out = total[:, :HEAD_DIM] / total[:, HEAD_DIM:]
        for i in range(count):
            g = first + i
            out_ref[:, :, g * HEAD_DIM : (g + 1) * HEAD_DIM] = (
                out[i * rows : (i + 1) * rows].astype(out_ref.dtype).reshape(blocks, rows_each, HEAD_DIM)
            )

    @pl.when(seen)
    def _():
        mine = kv_ref[:, :, 2 * HEAD_DIM :].reshape(n, HEAD_DIM)
        other = other_ref[...].reshape(n, HEAD_DIM)
        keys_here = core == 0
        k = jnp.where(keys_here, mine, other)
        v_ones = with_ones(jnp.where(keys_here, other, mine))
        firsts = range(0, GROUP, count)
        scores = [scores_of(head_rows(q_ref, first, count), k) for first in firsts]
        for first, block in zip(firsts, scores):
            at = slice(first * rows, (first + count) * rows)
            largest, sums = weigh(block, v_ones)
            before = largest_ref[at, :]
            after = jnp.maximum(before, largest)
            old = jnp.exp2((before - after) * BASE)
            new = jnp.exp2((largest - after) * BASE)
            old, new = jnp.concatenate([old, old], 1), jnp.concatenate([new, new], 1)
            store(first, sums_ref[at, :] * old + sums * new)

    @pl.when(jnp.logical_not(seen))
    def _():
        for first in range(0, GROUP, count):
            store(first, sums_ref[first * rows : (first + count) * rows, :])


def stage_kernel(query_ref, clean_key_ref, clean_value_ref, out_ref, mine_ref, sent_ref, sems):
    core = lax.axis_index("core")
    copies = [
        pltpu.make_async_copy(query_ref.at[0, :, pl.ds(h * WIDE, WIDE)], out_ref.at[h], sems.at[h])
        for h in range(KV_HEADS)
    ]
    for here, kept, given in ((0, clean_key_ref, clean_value_ref), (1, clean_value_ref, clean_key_ref)):

        @pl.when(core == here)
        def _():
            pltpu.make_async_copy(given.at[0], sent_ref, sems.at[KV_HEADS]).start()
            pltpu.make_async_copy(kept.at[0], mine_ref, sems.at[KV_HEADS + 1]).start()

    for copy in copies:
        copy.start()
    for copy in copies:
        copy.wait()
    pltpu.make_async_copy(clean_key_ref.at[0], sent_ref, sems.at[KV_HEADS]).wait()
    pltpu.make_async_copy(clean_key_ref.at[0], mine_ref, sems.at[KV_HEADS + 1]).wait()


def pair_kernel(key_ref, value_ref, out_ref, key_buf, value_buf, sems):
    copies = [
        pltpu.make_async_copy(key_ref.at[0], key_buf, sems.at[0]),
        pltpu.make_async_copy(value_ref.at[0], value_buf, sems.at[1]),
    ]
    for copy in copies:
        copy.start()
    for copy in copies:
        copy.wait()
    for h in range(KV_HEADS):
        at = slice(h * HEAD_DIM, (h + 1) * HEAD_DIM)
        first = (h % 2) * 2 * HEAD_DIM
        out_ref[h // 2, :, first : first + HEAD_DIM] = key_buf[:, at]
        out_ref[h // 2, :, first + HEAD_DIM : first + 2 * HEAD_DIM] = value_buf[:, at]


def pack_keys_kernel(completing_ref, pairs_ref, picked_ref, handed_ref, after_ref, out_ref):
    del after_ref
    handed = jnp.logical_and(lax.axis_index("half") == 1, completing_ref[0] < 2)
    clean = jnp.where(handed, handed_ref[...], picked_ref[...])
    for h in range(KV_HEADS):
        first = (h % 2) * 3 * HEAD_DIM
        near = pairs_ref[h // 2, :, (h % 2) * 2 * HEAD_DIM : (h % 2 + 1) * 2 * HEAD_DIM]
        for z in (h // 2, h // 2 + KV_HEADS // 2):
            out_ref[z, :, first : first + 2 * HEAD_DIM] = near
            out_ref[z, :, first + 2 * HEAD_DIM : first + 3 * HEAD_DIM] = clean[:, h * HEAD_DIM : (h + 1) * HEAD_DIM]


def spread_kernel(served_ref, out_ref):
    rows = served_ref.shape[0] * served_ref.shape[1]
    each = 3 * HEAD_DIM
    for i in range(out_ref.shape[0]):
        head = (i // 4) % 2
        out_ref[i] = served_ref[:, :, head * each : (head + 1) * each].reshape(rows, each)


def estimate(q_rows, n):
    return pl.CostEstimate(flops=4 * q_rows * n * HEAD_DIM, bytes_accessed=4 * 2**20, transcendentals=q_rows * n)


def call(kernel, out_shape, specs, *operands, cost=None):
    outs = (VMEM,) * len(out_shape) if isinstance(out_shape, tuple) else VMEM
    return pl.pallas_call(
        kernel,
        out_shape=out_shape,
        in_specs=specs,
        out_specs=outs,
        cost_estimate=cost,
        compiler_params=pltpu.CompilerParams(vmem_limit_bytes=40 * 2**20),
    )(*operands)


def shaped(*shape, dtype=jnp.bfloat16):
    return jax.ShapeDtypeStruct(shape, dtype)


def shards(query, key, value, clean_key, clean_value, completing, span_mask):
    tok = query.shape[1]
    heads = KV_HEADS
    z_all, served_by, plane_axes = ("zq", "zc"), ("zc", "xb"), ("xa", "xb", "y")
    depth, plane = 8, 16
    anywhere = pl.BlockSpec(memory_space=pl.ANY)

    width = heads * HEAD_DIM
    packed, mine, sent = pl.pallas_call(
        stage_kernel,
        out_shape=(shaped(heads, tok, WIDE), shaped(tok, width), shaped(tok, width)),
        in_specs=[anywhere] * 3,
        out_specs=(VMEM,) * 3,
        scratch_shapes=[pltpu.SemaphoreType.DMA((heads + 2,))],
    )(query, clean_key, clean_value)
    pairs = pl.pallas_call(
        pair_kernel,
        out_shape=shaped(heads // 2, tok, 4 * HEAD_DIM),
        in_specs=[anywhere] * 2,
        out_specs=VMEM,
        scratch_shapes=[pltpu.VMEM((tok, width), jnp.bfloat16)] * 2 + [pltpu.SemaphoreType.DMA((2,))],
        compiler_params=pltpu.CompilerParams(vmem_limit_bytes=40 * 2**20),
    )(key, value)
    served = lax.all_to_all(packed, served_by, 0, 0, tiled=True)

    swapped = lax.ppermute(sent, "core", [(0, 1), (1, 0)])
    picked = jnp.where(completing[0] % 2 == lax.axis_index("core"), mine, swapped)
    handed = lax.ppermute(
        picked, ("half",) + z_all, [(z, depth + (z + depth // 2) % depth) for z in range(depth)]
    )

    kv = call(
        pack_keys_kernel,
        shaped(depth, tok, 6 * HEAD_DIM),
        [SMEM] + [VMEM] * 3 + [anywhere],
        completing,
        pairs,
        picked,
        handed,
        served,
    )
    kv = lax.all_to_all(kv, z_all, 0, 0, tiled=True)
    kv = call(spread_kernel, shaped(plane, depth * tok, 3 * HEAD_DIM), [VMEM], kv)
    kv = lax.all_to_all(kv, plane_axes, 0, 0, tiled=True)
    other = lax.ppermute(kv[:, :, 2 * HEAD_DIM :], "core", [(0, 1), (1, 0)])

    rows, n = heads * tok * GROUP, plane * depth * tok
    sums, largest = call(
        functools.partial(own_kernel, 3),
        (shaped(rows, 2 * HEAD_DIM, dtype=jnp.float32), shaped(rows, HEAD_DIM, dtype=jnp.float32)),
        [VMEM] * 2,
        served,
        kv,
        cost=estimate(rows, n),
    )
    out = call(
        functools.partial(far_kernel, 3),
        shaped(heads, tok, WIDE),
        [SMEM] * 2 + [VMEM] * 5,
        completing,
        span_mask,
        served,
        kv,
        other,
        sums,
        largest,
        cost=estimate(rows, n),
    )
    out = lax.all_to_all(out, served_by, 0, 0, tiled=True)
    return jnp.transpose(out, (1, 0, 2)).reshape(1, tok, HEADS * HEAD_DIM)


def solution(mesh):
    grid = Mesh(mesh.devices.reshape(2, 2, 2, 4, 2, 2, 4), ("half", "core", "zq", "zc", "xa", "xb", "y"))
    rows = P(("half", "core"), ("zq", "zc", "xa", "xb", "y"), None)
    return jax.shard_map(
        shards, mesh=grid, in_specs=(rows,) * 5 + (P(), P()), out_specs=rows, check_vma=False
    )
```

```python
import functools
import math

import jax
import jax.numpy as jnp
from jax import lax
from jax.experimental import pallas as pl
from jax.experimental.pallas import tpu as pltpu
from jax.sharding import Mesh
from jax.sharding import PartitionSpec as P

HEAD_DIM = 128
HEADS = 48
KV_HEADS = 8
GROUP = HEADS // KV_HEADS
WIDE = GROUP * HEAD_DIM
BASE = HEAD_DIM**-0.5 * math.log2(math.e)
VMEM = pl.BlockSpec(memory_space=pltpu.VMEM)
SMEM = pl.BlockSpec(memory_space=pltpu.SMEM)


def head_rows(q_ref, first, count):
    rows = q_ref.shape[0] * q_ref.shape[1]
    return jnp.concatenate(
        [
            q_ref[:, :, g * HEAD_DIM : (g + 1) * HEAD_DIM].reshape(rows, HEAD_DIM)
            for g in range(first, first + count)
        ],
        0,
    )


def scores_of(q, k):
    return lax.dot_general(q, k, (((1,), (1,)), ((), ())), preferred_element_type=jnp.float32)


def weigh(scores, v_ones):
    largest = jnp.max(scores, axis=-1, keepdims=True)
    weights = jnp.exp2((scores - largest) * BASE).astype(jnp.bfloat16)
    return largest, jnp.dot(weights, v_ones, preferred_element_type=jnp.float32)


def with_ones(v):
    return jnp.concatenate([v, jnp.ones_like(v)], 1)


def own_kernel(count, q_ref, kv_ref, sums_ref, largest_ref):
    n = kv_ref.shape[0] * kv_ref.shape[1]
    rows = q_ref.shape[0] * q_ref.shape[1]
    k = kv_ref[:, :, :HEAD_DIM].reshape(n, HEAD_DIM)
    v_ones = with_ones(kv_ref[:, :, HEAD_DIM : 2 * HEAD_DIM].reshape(n, HEAD_DIM))
    firsts = range(0, GROUP, count)
    scores = [scores_of(head_rows(q_ref, first, count), k) for first in firsts]
    for first, block in zip(firsts, scores):
        at = slice(first * rows, (first + count) * rows)
        largest, sums = weigh(block, v_ones)
        sums_ref[at, :] = sums
        largest_ref[at, :] = jnp.broadcast_to(largest, (count * rows, HEAD_DIM))


def far_kernel(count, completing_ref, mask_ref, q_ref, kv_ref, other_ref, sums_ref, largest_ref, out_ref):
    n = kv_ref.shape[0] * kv_ref.shape[1]
    blocks, rows_each = q_ref.shape[0], q_ref.shape[1]
    rows = blocks * rows_each
    core = lax.axis_index("core")
    section = lax.axis_index("half") * 2 + core
    finished = completing_ref[0]
    seen = jnp.logical_and(section > finished, mask_ref[section, finished] == 1)

    def store(first, total):
        out = total[:, :HEAD_DIM] / total[:, HEAD_DIM:]
        for i in range(count):
            g = first + i
            out_ref[:, :, g * HEAD_DIM : (g + 1) * HEAD_DIM] = (
                out[i * rows : (i + 1) * rows].astype(out_ref.dtype).reshape(blocks, rows_each, HEAD_DIM)
            )

    @pl.when(seen)
    def _():
        mine = kv_ref[:, :, 2 * HEAD_DIM :].reshape(n, HEAD_DIM)
        other = other_ref[...].reshape(n, HEAD_DIM)
        keys_here = core == 0
        k = jnp.where(keys_here, mine, other)
        v_ones = with_ones(jnp.where(keys_here, other, mine))
        firsts = range(0, GROUP, count)
        scores = [scores_of(head_rows(q_ref, first, count), k) for first in firsts]
        for first, block in zip(firsts, scores):
            at = slice(first * rows, (first + count) * rows)
            largest, sums = weigh(block, v_ones)
            before = largest_ref[at, :]
            after = jnp.maximum(before, largest)
            old = jnp.exp2((before - after) * BASE)
            new = jnp.exp2((largest - after) * BASE)
            old, new = jnp.concatenate([old, old], 1), jnp.concatenate([new, new], 1)
            store(first, sums_ref[at, :] * old + sums * new)

    @pl.when(jnp.logical_not(seen))
    def _():
        for first in range(0, GROUP, count):
            store(first, sums_ref[first * rows : (first + count) * rows, :])


def stage_kernel(query_ref, clean_key_ref, clean_value_ref, keep_ref, send_ref, mine_ref, sent_ref, sems):
    core, xb = lax.axis_index("core"), lax.axis_index("xb")
    copies = []
    for z in range(KV_HEADS // 2):
        for i, (target, x) in enumerate(((keep_ref, xb), (send_ref, 1 - xb))):
            at = pl.ds(pl.multiple_of((2 * z + x) * WIDE, WIDE), WIDE)
            copies.append(pltpu.make_async_copy(query_ref.at[0, :, at], target.at[z], sems.at[2 * z + i]))
    for here, kept, given in ((0, clean_key_ref, clean_value_ref), (1, clean_value_ref, clean_key_ref)):

        @pl.when(core == here)
        def _():
            pltpu.make_async_copy(given.at[0], sent_ref, sems.at[KV_HEADS]).start()
            pltpu.make_async_copy(kept.at[0], mine_ref, sems.at[KV_HEADS + 1]).start()

    for copy in copies:
        copy.start()
    for copy in copies:
        copy.wait()
    pltpu.make_async_copy(clean_key_ref.at[0], sent_ref, sems.at[KV_HEADS]).wait()
    pltpu.make_async_copy(clean_key_ref.at[0], mine_ref, sems.at[KV_HEADS + 1]).wait()


def second_kernel(kept_ref, got_ref, keep_ref, send_ref):
    xb, low = lax.axis_index("xb"), lax.rem(lax.axis_index("zc"), 2)
    for source, x in ((kept_ref, xb), (got_ref, 1 - xb)):
        for high in range(2):
            keep_ref[x, high] = source[2 * high + low]
            send_ref[x, high] = source[2 * high + 1 - low]


def third_kernel(kept_ref, got_ref, keep_ref, send_ref):
    zc = lax.axis_index("zc")
    low, high = lax.rem(zc, 2), lax.div(zc, 2)
    for source, z in ((kept_ref, low), (got_ref, 1 - low)):
        for x in range(2):
            keep_ref[z, x] = source[x, high]
            send_ref[z, x] = source[x, 1 - high]


def last_kernel(kept_ref, got_ref, out_ref):
    high = lax.div(lax.axis_index("zc"), 2)
    for source, z in ((kept_ref, high), (got_ref, 1 - high)):
        for low in range(2):
            for x in range(2):
                out_ref[4 * z + 2 * low + x] = source[low, x]


def pair_kernel(key_ref, value_ref, out_ref, key_buf, value_buf, sems):
    copies = [
        pltpu.make_async_copy(key_ref.at[0], key_buf, sems.at[0]),
        pltpu.make_async_copy(value_ref.at[0], value_buf, sems.at[1]),
    ]
    for copy in copies:
        copy.start()
    for copy in copies:
        copy.wait()
    for h in range(KV_HEADS):
        at = slice(h * HEAD_DIM, (h + 1) * HEAD_DIM)
        first = (h % 2) * 2 * HEAD_DIM
        out_ref[h // 2, :, first : first + HEAD_DIM] = key_buf[:, at]
        out_ref[h // 2, :, first + HEAD_DIM : first + 2 * HEAD_DIM] = value_buf[:, at]


def pack_keys_kernel(completing_ref, pairs_ref, picked_ref, handed_ref, out_ref):
    handed = jnp.logical_and(lax.axis_index("half") == 1, completing_ref[0] < 2)
    clean = jnp.where(handed, handed_ref[...], picked_ref[...])
    for h in range(KV_HEADS):
        first = (h % 2) * 3 * HEAD_DIM
        near = pairs_ref[h // 2, :, (h % 2) * 2 * HEAD_DIM : (h % 2 + 1) * 2 * HEAD_DIM]
        for z in (h // 2, h // 2 + KV_HEADS // 2):
            out_ref[z, :, first : first + 2 * HEAD_DIM] = near
            out_ref[z, :, first + 2 * HEAD_DIM : first + 3 * HEAD_DIM] = clean[:, h * HEAD_DIM : (h + 1) * HEAD_DIM]


def spread_kernel(served_ref, after_ref, out_ref):
    del after_ref
    rows = served_ref.shape[0] * served_ref.shape[1]
    each = 3 * HEAD_DIM
    for i in range(out_ref.shape[0]):
        head = (i // 4) % 2
        out_ref[i] = served_ref[:, :, head * each : (head + 1) * each].reshape(rows, each)


def clean_kernel(kv_ref, after_ref, out_ref):
    del after_ref
    out_ref[...] = kv_ref[:, :, 2 * HEAD_DIM :]


def estimate(q_rows, n):
    return pl.CostEstimate(flops=4 * q_rows * n * HEAD_DIM, bytes_accessed=4 * 2**20, transcendentals=q_rows * n)


def call(kernel, out_shape, specs, *operands, cost=None):
    outs = (VMEM,) * len(out_shape) if isinstance(out_shape, tuple) else VMEM
    return pl.pallas_call(
        kernel,
        out_shape=out_shape,
        in_specs=specs,
        out_specs=outs,
        cost_estimate=cost,
        compiler_params=pltpu.CompilerParams(vmem_limit_bytes=40 * 2**20),
    )(*operands)


def shaped(*shape, dtype=jnp.bfloat16):
    return jax.ShapeDtypeStruct(shape, dtype)


def shards(query, key, value, clean_key, clean_value, completing, span_mask):
    tok = query.shape[1]
    heads = KV_HEADS
    z_all, served_by, plane_axes = ("zq", "zc"), ("zc", "xb"), ("xa", "xb", "y")
    depth, plane = 8, 16
    anywhere = pl.BlockSpec(memory_space=pl.ANY)

    width = heads * HEAD_DIM
    part = heads // 2
    keep, send, mine, sent = pl.pallas_call(
        stage_kernel,
        out_shape=(shaped(part, tok, WIDE),) * 2 + (shaped(tok, width),) * 2,
        in_specs=[anywhere] * 3,
        out_specs=(VMEM,) * 4,
        scratch_shapes=[pltpu.SemaphoreType.DMA((heads + 2,))],
    )(query, clean_key, clean_value)
    got = lax.ppermute(send, "xb", [(0, 1), (1, 0)])
    halves = (shaped(2, 2, tok, WIDE),) * 2
    keep, send = call(second_kernel, halves, [VMEM] * 2, keep, got)
    after_first = keep
    got = lax.ppermute(send, "zc", [(z, z ^ 1) for z in range(4)])
    keep, send = call(third_kernel, halves, [VMEM] * 2, keep, got)
    got = lax.ppermute(send, "zc", [(z, z ^ 2) for z in range(4)])
    served = call(last_kernel, shaped(heads, tok, WIDE), [VMEM] * 2, keep, got)

    pairs = pl.pallas_call(
        pair_kernel,
        out_shape=shaped(heads // 2, tok, 4 * HEAD_DIM),
        in_specs=[anywhere] * 2,
        out_specs=VMEM,
        scratch_shapes=[pltpu.VMEM((tok, width), jnp.bfloat16)] * 2 + [pltpu.SemaphoreType.DMA((2,))],
        compiler_params=pltpu.CompilerParams(vmem_limit_bytes=40 * 2**20),
    )(key, value)

    swapped = lax.ppermute(sent, "core", [(0, 1), (1, 0)])
    picked = jnp.where(completing[0] % 2 == lax.axis_index("core"), mine, swapped)
    handed = lax.ppermute(
        picked, ("half",) + z_all, [(z, depth + (z + depth // 2) % depth) for z in range(depth)]
    )

    kv = call(
        pack_keys_kernel,
        shaped(depth, tok, 6 * HEAD_DIM),
        [SMEM] + [VMEM] * 3,
        completing,
        pairs,
        picked,
        handed,
    )
    kv = lax.all_to_all(kv, z_all, 0, 0, tiled=True)
    kv = call(spread_kernel, shaped(plane, depth * tok, 3 * HEAD_DIM), [VMEM, anywhere], kv, after_first)
    kv = lax.all_to_all(kv, plane_axes, 0, 0, tiled=True)
    clean = call(clean_kernel, shaped(plane, depth * tok, HEAD_DIM), [VMEM, anywhere], kv, served)
    other = lax.ppermute(clean, "core", [(0, 1), (1, 0)])

    rows, n = heads * tok * GROUP, plane * depth * tok
    sums, largest = call(
        functools.partial(own_kernel, 3),
        (shaped(rows, 2 * HEAD_DIM, dtype=jnp.float32), shaped(rows, HEAD_DIM, dtype=jnp.float32)),
        [VMEM] * 2,
        served,
        kv,
        cost=estimate(rows, n),
    )
    out = call(
        functools.partial(far_kernel, 3),
        shaped(heads, tok, WIDE),
        [SMEM] * 2 + [VMEM] * 5,
        completing,
        span_mask,
        served,
        kv,
        other,
        sums,
        largest,
        cost=estimate(rows, n),
    )
    out = lax.all_to_all(out, served_by, 0, 0, tiled=True)
    return jnp.transpose(out, (1, 0, 2)).reshape(1, tok, HEADS * HEAD_DIM)


def solution(mesh):
    grid = Mesh(mesh.devices.reshape(2, 2, 2, 4, 2, 2, 4), ("half", "core", "zq", "zc", "xa", "xb", "y"))
    rows = P(("half", "core"), ("zq", "zc", "xa", "xb", "y"), None)
    return jax.shard_map(
        shards, mesh=grid, in_specs=(rows,) * 5 + (P(), P()), out_specs=rows, check_vma=False
    )
```

```python
import functools
import math

import jax
import jax.numpy as jnp
from jax import lax
from jax.experimental import pallas as pl
from jax.experimental.pallas import tpu as pltpu
from jax.sharding import Mesh
from jax.sharding import PartitionSpec as P

HEAD_DIM = 128
HEADS = 48
KV_HEADS = 8
GROUP = HEADS // KV_HEADS
WIDE = GROUP * HEAD_DIM
BASE = HEAD_DIM**-0.5 * math.log2(math.e)
VMEM = pl.BlockSpec(memory_space=pltpu.VMEM)
SMEM = pl.BlockSpec(memory_space=pltpu.SMEM)


def head_rows(q_ref, first, count):
    rows = q_ref.shape[0] * q_ref.shape[1]
    return jnp.concatenate(
        [
            q_ref[:, :, g * HEAD_DIM : (g + 1) * HEAD_DIM].reshape(rows, HEAD_DIM)
            for g in range(first, first + count)
        ],
        0,
    )


def scores_of(q, k):
    return lax.dot_general(q, k, (((1,), (1,)), ((), ())), preferred_element_type=jnp.float32)


def weigh(scores, v_ones):
    largest = jnp.max(scores, axis=-1, keepdims=True)
    weights = jnp.exp2((scores - largest) * BASE).astype(jnp.bfloat16)
    return largest, jnp.dot(weights, v_ones, preferred_element_type=jnp.float32)


def with_ones(v):
    return jnp.concatenate([v, jnp.ones_like(v)], 1)


def own_kernel(count, q_ref, kv_ref, sums_ref, largest_ref):
    n = kv_ref.shape[0] * kv_ref.shape[1]
    rows = q_ref.shape[0] * q_ref.shape[1]
    k = kv_ref[:, :, :HEAD_DIM].reshape(n, HEAD_DIM)
    v_ones = with_ones(kv_ref[:, :, HEAD_DIM : 2 * HEAD_DIM].reshape(n, HEAD_DIM))
    firsts = range(0, GROUP, count)
    scores = [scores_of(head_rows(q_ref, first, count), k) for first in firsts]
    for first, block in zip(firsts, scores):
        at = slice(first * rows, (first + count) * rows)
        largest, sums = weigh(block, v_ones)
        sums_ref[at, :] = sums
        largest_ref[at, :] = jnp.broadcast_to(largest, (count * rows, HEAD_DIM))


def far_kernel(count, completing_ref, mask_ref, q_ref, kv_ref, other_ref, sums_ref, largest_ref, out_ref):
    n = kv_ref.shape[0] * kv_ref.shape[1]
    blocks, rows_each = q_ref.shape[0], q_ref.shape[1]
    rows = blocks * rows_each
    core = lax.axis_index("core")
    section = lax.axis_index("half") * 2 + core
    finished = completing_ref[0]
    seen = jnp.logical_and(section > finished, mask_ref[section, finished] == 1)

    def store(first, total):
        out = total[:, :HEAD_DIM] / total[:, HEAD_DIM:]
        for i in range(count):
            g = first + i
            out_ref[:, :, g * HEAD_DIM : (g + 1) * HEAD_DIM] = (
                out[i * rows : (i + 1) * rows].astype(out_ref.dtype).reshape(blocks, rows_each, HEAD_DIM)
            )

    @pl.when(seen)
    def _():
        mine = kv_ref[:, :, 2 * HEAD_DIM :].reshape(n, HEAD_DIM)
        other = other_ref[...].reshape(n, HEAD_DIM)
        keys_here = core == 0
        k = jnp.where(keys_here, mine, other)
        v_ones = with_ones(jnp.where(keys_here, other, mine))
        firsts = range(0, GROUP, count)
        scores = [scores_of(head_rows(q_ref, first, count), k) for first in firsts]
        for first, block in zip(firsts, scores):
            at = slice(first * rows, (first + count) * rows)
            largest, sums = weigh(block, v_ones)
            before = largest_ref[at, :]
            after = jnp.maximum(before, largest)
            old = jnp.exp2((before - after) * BASE)
            new = jnp.exp2((largest - after) * BASE)
            old, new = jnp.concatenate([old, old], 1), jnp.concatenate([new, new], 1)
            store(first, sums_ref[at, :] * old + sums * new)

    @pl.when(jnp.logical_not(seen))
    def _():
        for first in range(0, GROUP, count):
            store(first, sums_ref[first * rows : (first + count) * rows, :])


def stage_kernel(query_ref, after_ref, keep_ref, send_ref, sems):
    del after_ref
    xb = lax.axis_index("xb")
    copies = []
    for z in range(KV_HEADS // 2):
        for i, (target, x) in enumerate(((keep_ref, xb), (send_ref, 1 - xb))):
            at = pl.ds(pl.multiple_of((2 * z + x) * WIDE, WIDE), WIDE)
            copies.append(pltpu.make_async_copy(query_ref.at[0, :, at], target.at[z], sems.at[2 * z + i]))
    for copy in copies:
        copy.start()
    for copy in copies:
        copy.wait()


def second_kernel(kept_ref, got_ref, keep_ref, send_ref):
    xb, low = lax.axis_index("xb"), lax.rem(lax.axis_index("zc"), 2)
    for source, x in ((kept_ref, xb), (got_ref, 1 - xb)):
        for high in range(2):
            keep_ref[x, high] = source[2 * high + low]
            send_ref[x, high] = source[2 * high + 1 - low]


def third_kernel(kept_ref, got_ref, keep_ref, send_ref):
    zc = lax.axis_index("zc")
    low, high = lax.rem(zc, 2), lax.div(zc, 2)
    for source, z in ((kept_ref, low), (got_ref, 1 - low)):
        for x in range(2):
            keep_ref[z, x] = source[x, high]
            send_ref[z, x] = source[x, 1 - high]


def last_kernel(kept_ref, got_ref, out_ref):
    high = lax.div(lax.axis_index("zc"), 2)
    for source, z in ((kept_ref, high), (got_ref, 1 - high)):
        for low in range(2):
            for x in range(2):
                out_ref[4 * z + 2 * low + x] = source[low, x]


def pair_kernel(key_ref, value_ref, sent_ref, after_ref, out_ref, late_ref, key_buf, value_buf, sems):
    del after_ref
    late_ref[...] = sent_ref[...]
    copies = [
        pltpu.make_async_copy(key_ref.at[0], key_buf, sems.at[0]),
        pltpu.make_async_copy(value_ref.at[0], value_buf, sems.at[1]),
    ]
    for copy in copies:
        copy.start()
    for copy in copies:
        copy.wait()
    for h in range(KV_HEADS):
        at = slice(h * HEAD_DIM, (h + 1) * HEAD_DIM)
        first = (h % 2) * 2 * HEAD_DIM
        out_ref[h // 2, :, first : first + HEAD_DIM] = key_buf[:, at]
        out_ref[h // 2, :, first + HEAD_DIM : first + 2 * HEAD_DIM] = value_buf[:, at]


def pack_keys_kernel(completing_ref, pairs_ref, picked_ref, late_ref, handed_ref, out_ref):
    upper = lax.axis_index("half") == 1
    handed = jnp.logical_and(upper, completing_ref[0] < 2)
    late = jnp.logical_and(upper, lax.axis_index("core") == 1)
    clean = jnp.where(handed, handed_ref[...], jnp.where(late, late_ref[...], picked_ref[...]))
    for h in range(KV_HEADS):
        first = (h % 2) * 3 * HEAD_DIM
        near = pairs_ref[h // 2, :, (h % 2) * 2 * HEAD_DIM : (h % 2 + 1) * 2 * HEAD_DIM]
        for z in (h // 2, h // 2 + KV_HEADS // 2):
            out_ref[z, :, first : first + 2 * HEAD_DIM] = near
            out_ref[z, :, first + 2 * HEAD_DIM : first + 3 * HEAD_DIM] = clean[:, h * HEAD_DIM : (h + 1) * HEAD_DIM]


def spread_kernel(served_ref, after_ref, out_ref):
    del after_ref
    rows = served_ref.shape[0] * served_ref.shape[1]
    each = 3 * HEAD_DIM
    for i in range(out_ref.shape[0]):
        head = (i // 4) % 2
        out_ref[i] = served_ref[:, :, head * each : (head + 1) * each].reshape(rows, each)


def clean_kernel(kv_ref, after_ref, out_ref):
    del after_ref
    out_ref[...] = kv_ref[:, :, 2 * HEAD_DIM :]


def estimate(q_rows, n):
    return pl.CostEstimate(flops=4 * q_rows * n * HEAD_DIM, bytes_accessed=4 * 2**20, transcendentals=q_rows * n)


def call(kernel, out_shape, specs, *operands, cost=None, mib=16):
    outs = (VMEM,) * len(out_shape) if isinstance(out_shape, tuple) else VMEM
    return pl.pallas_call(
        kernel,
        out_shape=out_shape,
        in_specs=specs,
        out_specs=outs,
        cost_estimate=cost,
        compiler_params=pltpu.CompilerParams(vmem_limit_bytes=mib * 2**20),
    )(*operands)


def shaped(*shape, dtype=jnp.bfloat16):
    return jax.ShapeDtypeStruct(shape, dtype)


def shards(query, key, value, clean_key, clean_value, completing, span_mask):
    tok = query.shape[1]
    heads = KV_HEADS
    z_all, served_by, plane_axes = ("zq", "zc"), ("zc", "xb"), ("xa", "xb", "y")
    depth, plane = 8, 16
    anywhere = pl.BlockSpec(memory_space=pl.ANY)

    width = heads * HEAD_DIM
    core = lax.axis_index("core")
    mine = jnp.where(core == 0, clean_key[0], clean_value[0])
    sent = jnp.where(core == 0, clean_value[0], clean_key[0])
    swapped = lax.ppermute(sent, ("half", "core"), [(0, 1), (1, 0)])
    picked = jnp.where(completing[0] % 2 == core, mine, swapped)
    handed = lax.ppermute(
        picked, ("half",) + z_all, [(z, depth + (z + depth // 2) % depth) for z in range(depth)]
    )
    pairs, late = pl.pallas_call(
        pair_kernel,
        out_shape=(shaped(heads // 2, tok, 4 * HEAD_DIM), shaped(tok, width)),
        in_specs=[anywhere] * 2 + [VMEM, anywhere],
        out_specs=(VMEM,) * 2,
        scratch_shapes=[pltpu.VMEM((tok, width), jnp.bfloat16)] * 2 + [pltpu.SemaphoreType.DMA((2,))],
        compiler_params=pltpu.CompilerParams(vmem_limit_bytes=16 * 2**20),
    )(key, value, sent, picked)
    late = lax.ppermute(late, ("half", "core"), [(2, 3)])

    kv = call(
        pack_keys_kernel,
        shaped(depth, tok, 6 * HEAD_DIM),
        [SMEM] + [VMEM] * 4,
        completing,
        pairs,
        picked,
        late,
        handed,
    )
    part = heads // 2
    keep, send = pl.pallas_call(
        stage_kernel,
        out_shape=(shaped(part, tok, WIDE),) * 2,
        in_specs=[anywhere] * 2,
        out_specs=(VMEM,) * 2,
        scratch_shapes=[pltpu.SemaphoreType.DMA((heads,))],
        compiler_params=pltpu.CompilerParams(vmem_limit_bytes=16 * 2**20),
    )(query, kv)
    got = lax.ppermute(send, "xb", [(0, 1), (1, 0)])
    halves = (shaped(2, 2, tok, WIDE),) * 2
    keep, send = call(second_kernel, halves, [VMEM] * 2, keep, got)
    after_first = keep
    got = lax.ppermute(send, "zc", [(z, z ^ 1) for z in range(4)])
    keep, send = call(third_kernel, halves, [VMEM] * 2, keep, got)
    got = lax.ppermute(send, "zc", [(z, z ^ 2) for z in range(4)])
    served = call(last_kernel, shaped(heads, tok, WIDE), [VMEM] * 2, keep, got)


    kv = lax.all_to_all(kv, z_all, 0, 0, tiled=True)
    kv = call(spread_kernel, shaped(plane, depth * tok, 3 * HEAD_DIM), [VMEM, anywhere], kv, after_first)
    kv = lax.all_to_all(kv, plane_axes, 0, 0, tiled=True)
    clean = call(clean_kernel, shaped(plane, depth * tok, HEAD_DIM), [VMEM, anywhere], kv, served)
    other = lax.ppermute(clean, "core", [(0, 1), (1, 0)])

    rows, n = heads * tok * GROUP, plane * depth * tok
    sums, largest = call(
        functools.partial(own_kernel, 3),
        (shaped(rows, 2 * HEAD_DIM, dtype=jnp.float32), shaped(rows, HEAD_DIM, dtype=jnp.float32)),
        [VMEM] * 2,
        served,
        kv,
        cost=estimate(rows, n),
        mib=40,
    )
    out = call(
        functools.partial(far_kernel, 3),
        shaped(heads, tok, WIDE),
        [SMEM] * 2 + [VMEM] * 5,
        completing,
        span_mask,
        served,
        kv,
        other,
        sums,
        largest,
        cost=estimate(rows, n),
        mib=40,
    )
    out = lax.all_to_all(out, served_by, 0, 0, tiled=True)
    return jnp.transpose(out, (1, 0, 2)).reshape(1, tok, HEADS * HEAD_DIM)


def solution(mesh):
    grid = Mesh(mesh.devices.reshape(2, 2, 2, 4, 2, 2, 4), ("half", "core", "zq", "zc", "xa", "xb", "y"))
    rows = P(("half", "core"), ("zq", "zc", "xa", "xb", "y"), None)
    return jax.shard_map(
        shards, mesh=grid, in_specs=(rows,) * 5 + (P(), P()), out_specs=rows, check_vma=False
    )
```

```python
import functools
import math

import jax
import jax.numpy as jnp
from jax import lax
from jax.experimental import pallas as pl
from jax.experimental.pallas import tpu as pltpu
from jax.sharding import Mesh
from jax.sharding import PartitionSpec as P

HEAD_DIM = 128
HEADS = 48
KV_HEADS = 8
GROUP = HEADS // KV_HEADS
WIDE = GROUP * HEAD_DIM
BASE = HEAD_DIM**-0.5 * math.log2(math.e)
VMEM = pl.BlockSpec(memory_space=pltpu.VMEM)
SMEM = pl.BlockSpec(memory_space=pltpu.SMEM)


def head_rows(q_ref, first, count):
    rows = q_ref.shape[0] * q_ref.shape[1]
    return jnp.concatenate(
        [
            q_ref[:, :, g * HEAD_DIM : (g + 1) * HEAD_DIM].reshape(rows, HEAD_DIM)
            for g in range(first, first + count)
        ],
        0,
    )


def scores_of(q, k):
    return lax.dot_general(q, k, (((1,), (1,)), ((), ())), preferred_element_type=jnp.float32)


def weigh(scores, v_ones):
    largest = jnp.max(scores, axis=-1, keepdims=True)
    weights = jnp.exp2((scores - largest) * BASE).astype(jnp.bfloat16)
    return largest, jnp.dot(weights, v_ones, preferred_element_type=jnp.float32)


def with_ones(v):
    return jnp.concatenate([v, jnp.ones_like(v)], 1)


def own_kernel(count, q_ref, kv_ref, sums_ref, largest_ref):
    n = kv_ref.shape[0] * kv_ref.shape[1]
    rows = q_ref.shape[0] * q_ref.shape[1]
    k = kv_ref[:, :, :HEAD_DIM].reshape(n, HEAD_DIM)
    v_ones = with_ones(kv_ref[:, :, HEAD_DIM : 2 * HEAD_DIM].reshape(n, HEAD_DIM))
    firsts = range(0, GROUP, count)
    scores = [scores_of(head_rows(q_ref, first, count), k) for first in firsts]
    for first, block in zip(firsts, scores):
        at = slice(first * rows, (first + count) * rows)
        largest, sums = weigh(block, v_ones)
        sums_ref[at, :] = sums
        largest_ref[at, :] = jnp.broadcast_to(largest, (count * rows, HEAD_DIM))


def far_kernel(count, completing_ref, mask_ref, q_ref, kv_ref, other_ref, sums_ref, largest_ref, out_ref):
    n = kv_ref.shape[0] * kv_ref.shape[1]
    blocks, rows_each = q_ref.shape[0], q_ref.shape[1]
    rows = blocks * rows_each
    core = lax.axis_index("core")
    section = lax.axis_index("half") * 2 + core
    finished = completing_ref[0]
    seen = jnp.logical_and(section > finished, mask_ref[section, finished] == 1)

    def store(first, total):
        out = total[:, :HEAD_DIM] / total[:, HEAD_DIM:]
        for i in range(count):
            g = first + i
            out_ref[:, :, g * HEAD_DIM : (g + 1) * HEAD_DIM] = (
                out[i * rows : (i + 1) * rows].astype(out_ref.dtype).reshape(blocks, rows_each, HEAD_DIM)
            )

    @pl.when(seen)
    def _():
        mine = kv_ref[:, :, 2 * HEAD_DIM :].reshape(n, HEAD_DIM)
        other = other_ref[...].reshape(n, HEAD_DIM)
        keys_here = core == 0
        k = jnp.where(keys_here, mine, other)
        v_ones = with_ones(jnp.where(keys_here, other, mine))
        firsts = range(0, GROUP, count)
        scores = [scores_of(head_rows(q_ref, first, count), k) for first in firsts]
        for first, block in zip(firsts, scores):
            at = slice(first * rows, (first + count) * rows)
            largest, sums = weigh(block, v_ones)
            before = largest_ref[at, :]
            after = jnp.maximum(before, largest)
            old = jnp.exp2((before - after) * BASE)
            new = jnp.exp2((largest - after) * BASE)
            old, new = jnp.concatenate([old, old], 1), jnp.concatenate([new, new], 1)
            store(first, sums_ref[at, :] * old + sums * new)

    @pl.when(jnp.logical_not(seen))
    def _():
        for first in range(0, GROUP, count):
            store(first, sums_ref[first * rows : (first + count) * rows, :])


def stage_kernel(query_ref, after_ref, keep_ref, send_ref, sems):
    del after_ref
    xb = lax.axis_index("xb")
    copies = []
    for z in range(KV_HEADS // 2):
        for i, (target, x) in enumerate(((keep_ref, xb), (send_ref, 1 - xb))):
            at = pl.ds(pl.multiple_of((2 * z + x) * WIDE, WIDE), WIDE)
            copies.append(pltpu.make_async_copy(query_ref.at[0, :, at], target.at[z], sems.at[2 * z + i]))
    for copy in copies:
        copy.start()
    for copy in copies:
        copy.wait()


def second_kernel(kept_ref, got_ref, keep_ref, send_ref):
    xb, low = lax.axis_index("xb"), lax.rem(lax.axis_index("zc"), 2)
    for source, x in ((kept_ref, xb), (got_ref, 1 - xb)):
        for high in range(2):
            keep_ref[x, high] = source[2 * high + low]
            send_ref[x, high] = source[2 * high + 1 - low]


def third_kernel(completing_ref, kept_ref, got_ref, keep_ref, send_ref):
    del completing_ref
    zc = lax.axis_index("zc")
    low, high = lax.rem(zc, 2), lax.div(zc, 2)
    for source, z in ((kept_ref, low), (got_ref, 1 - low)):
        for x in range(2):
            keep_ref[z, x] = source[x, high]
            send_ref[z, x] = source[x, 1 - high]


def last_kernel(kept_ref, got_ref, out_ref):
    high = lax.div(lax.axis_index("zc"), 2)
    for source, z in ((kept_ref, high), (got_ref, 1 - high)):
        for low in range(2):
            for x in range(2):
                out_ref[4 * z + 2 * low + x] = source[low, x]


def pair_kernel(near_ref, sent_ref, after_ref, out_ref, late_ref):
    del after_ref
    late_ref[...] = sent_ref[...]
    for h in range(KV_HEADS):
        at = slice(h * HEAD_DIM, (h + 1) * HEAD_DIM)
        first = (h % 2) * 2 * HEAD_DIM
        for i in range(2):
            out_ref[h // 2, :, first + i * HEAD_DIM : first + (i + 1) * HEAD_DIM] = near_ref[i, :, at]


def pick_kernel(completing_ref, mine_ref, swapped_ref, out_ref):
    other = lax.bitwise_and(completing_ref[...], 1) != lax.axis_index("core")
    out_ref[...] = jnp.where(jnp.broadcast_to(other, out_ref.shape), swapped_ref[...], mine_ref[...])


def pack_keys_kernel(completing_ref, pairs_ref, picked_ref, late_ref, handed_ref, out_ref):
    upper = lax.axis_index("half") == 1
    handed = jnp.broadcast_to(jnp.where(upper, completing_ref[...], 2) < 2, handed_ref.shape)
    late = jnp.logical_and(upper, lax.axis_index("core") == 1)
    clean = jnp.where(handed, handed_ref[...], jnp.where(late, late_ref[...], picked_ref[...]))
    for h in range(KV_HEADS):
        first = (h % 2) * 3 * HEAD_DIM
        near = pairs_ref[h // 2, :, (h % 2) * 2 * HEAD_DIM : (h % 2 + 1) * 2 * HEAD_DIM]
        for z in (h // 2, h // 2 + KV_HEADS // 2):
            out_ref[z, :, first : first + 2 * HEAD_DIM] = near
            out_ref[z, :, first + 2 * HEAD_DIM : first + 3 * HEAD_DIM] = clean[:, h * HEAD_DIM : (h + 1) * HEAD_DIM]


def spread_kernel(served_ref, after_ref, out_ref):
    del after_ref
    rows = served_ref.shape[0] * served_ref.shape[1]
    each = 3 * HEAD_DIM
    for i in range(out_ref.shape[0]):
        head = (i // 4) % 2
        out_ref[i] = served_ref[:, :, head * each : (head + 1) * each].reshape(rows, each)


def clean_kernel(kv_ref, after_ref, out_ref):
    del after_ref
    out_ref[...] = kv_ref[:, :, 2 * HEAD_DIM :]


def estimate(q_rows, n):
    return pl.CostEstimate(flops=4 * q_rows * n * HEAD_DIM, bytes_accessed=4 * 2**20, transcendentals=q_rows * n)


def call(kernel, out_shape, specs, *operands, cost=None, mib=16):
    outs = (VMEM,) * len(out_shape) if isinstance(out_shape, tuple) else VMEM
    return pl.pallas_call(
        kernel,
        out_shape=out_shape,
        in_specs=specs,
        out_specs=outs,
        cost_estimate=cost,
        compiler_params=pltpu.CompilerParams(vmem_limit_bytes=mib * 2**20),
    )(*operands)


def shaped(*shape, dtype=jnp.bfloat16):
    return jax.ShapeDtypeStruct(shape, dtype)


def shards(query, key, value, clean_key, clean_value, completing, span_mask):
    tok = query.shape[1]
    heads = KV_HEADS
    z_all, served_by, plane_axes = ("zq", "zc"), ("zc", "xb"), ("xa", "xb", "y")
    depth, plane = 8, 16
    anywhere = pl.BlockSpec(memory_space=pl.ANY)

    width = heads * HEAD_DIM
    core = lax.axis_index("core")
    mine = jnp.where(core == 0, clean_key[0], clean_value[0])
    near = jnp.stack([key[0], value[0]])
    sent = jnp.where(core == 0, clean_value[0], clean_key[0])
    swapped = lax.ppermute(sent, ("half", "core"), [(0, 1), (1, 0)])
    finished = completing.reshape(1, 1)
    picked = call(pick_kernel, shaped(tok, width), [VMEM] * 3, finished, mine, swapped)
    handed = lax.ppermute(
        picked, ("half",) + z_all, [(z, depth + (z + depth // 2) % depth) for z in range(depth)]
    )
    pairs, late = call(
        pair_kernel,
        (shaped(heads // 2, tok, 4 * HEAD_DIM), shaped(tok, width)),
        [VMEM] * 2 + [anywhere],
        near,
        sent,
        picked,
    )
    late = lax.ppermute(late, ("half", "core"), [(2, 3)])

    kv = call(
        pack_keys_kernel,
        shaped(depth, tok, 6 * HEAD_DIM),
        [VMEM] * 5,
        finished,
        pairs,
        picked,
        late,
        handed,
    )
    part = heads // 2
    keep, send = pl.pallas_call(
        stage_kernel,
        out_shape=(shaped(part, tok, WIDE),) * 2,
        in_specs=[anywhere] * 2,
        out_specs=(VMEM,) * 2,
        scratch_shapes=[pltpu.SemaphoreType.DMA((heads,))],
        compiler_params=pltpu.CompilerParams(vmem_limit_bytes=16 * 2**20),
    )(query, kv)
    got = lax.ppermute(send, "xb", [(0, 1), (1, 0)])
    halves = (shaped(2, 2, tok, WIDE),) * 2
    keep, send = call(second_kernel, halves, [VMEM] * 2, keep, got)
    after_first = keep
    got = lax.ppermute(send, "zc", [(z, z ^ 1) for z in range(4)])
    keep, send = call(third_kernel, halves, [SMEM] + [VMEM] * 2, completing, keep, got)
    got = lax.ppermute(send, "zc", [(z, z ^ 2) for z in range(4)])
    served = call(last_kernel, shaped(heads, tok, WIDE), [VMEM] * 2, keep, got)


    kv = lax.all_to_all(kv, z_all, 0, 0, tiled=True)
    kv = call(spread_kernel, shaped(plane, depth * tok, 3 * HEAD_DIM), [VMEM, anywhere], kv, after_first)
    kv = lax.all_to_all(kv, plane_axes, 0, 0, tiled=True)
    clean = call(clean_kernel, shaped(plane, depth * tok, HEAD_DIM), [VMEM, anywhere], kv, served)
    other = lax.ppermute(clean, "core", [(0, 1), (1, 0)])

    rows, n = heads * tok * GROUP, plane * depth * tok
    sums, largest = call(
        functools.partial(own_kernel, 3),
        (shaped(rows, 2 * HEAD_DIM, dtype=jnp.float32), shaped(rows, HEAD_DIM, dtype=jnp.float32)),
        [VMEM] * 2,
        served,
        kv,
        cost=estimate(rows, n),
        mib=40,
    )
    out = call(
        functools.partial(far_kernel, 3),
        shaped(heads, tok, WIDE),
        [SMEM] * 2 + [VMEM] * 5,
        completing,
        span_mask,
        served,
        kv,
        other,
        sums,
        largest,
        cost=estimate(rows, n),
        mib=40,
    )
    out = lax.all_to_all(out, served_by, 0, 0, tiled=True)
    return jnp.transpose(out, (1, 0, 2)).reshape(1, tok, HEADS * HEAD_DIM)


def solution(mesh):
    grid = Mesh(mesh.devices.reshape(2, 2, 2, 4, 2, 2, 4), ("half", "core", "zq", "zc", "xa", "xb", "y"))
    rows = P(("half", "core"), ("zq", "zc", "xa", "xb", "y"), None)
    return jax.shard_map(
        shards, mesh=grid, in_specs=(rows,) * 5 + (P(), P()), out_specs=rows, check_vma=False
    )
```

```python
import functools
import math

import jax
import jax.numpy as jnp
from jax import lax
from jax.experimental import pallas as pl
from jax.experimental.pallas import tpu as pltpu
from jax.sharding import Mesh
from jax.sharding import PartitionSpec as P

HEAD_DIM = 128
HEADS = 48
KV_HEADS = 8
GROUP = HEADS // KV_HEADS
WIDE = GROUP * HEAD_DIM
BASE = HEAD_DIM**-0.5 * math.log2(math.e)
Z_ORDER = [3, 4, 5, 6, 7, 0, 1, 2]
FIRST_ZC = 1
SERVE_ORDER = [(i + 2 * FIRST_ZC) % 8 for i in range(8)]
VMEM = pl.BlockSpec(memory_space=pltpu.VMEM)


def head_rows(q_ref, first, count):
    rows = q_ref.shape[0] * q_ref.shape[1]
    return jnp.concatenate(
        [
            q_ref[:, :, g * HEAD_DIM : (g + 1) * HEAD_DIM].reshape(rows, HEAD_DIM)
            for g in range(first, first + count)
        ],
        0,
    )


def scores_of(q, k):
    return lax.dot_general(q, k, (((1,), (1,)), ((), ())), preferred_element_type=jnp.float32)


def weigh(scores, v_ones):
    largest = jnp.max(scores, axis=-1, keepdims=True)
    weights = jnp.exp2((scores - largest) * BASE).astype(jnp.bfloat16)
    return largest, jnp.dot(weights, v_ones, preferred_element_type=jnp.float32)


def with_ones(v):
    return jnp.concatenate([v, jnp.ones_like(v)], 1)


def own_kernel(count, q_ref, kv_ref, sums_ref, largest_ref):
    n = kv_ref.shape[0] * kv_ref.shape[1]
    rows = q_ref.shape[0] * q_ref.shape[1]
    k = kv_ref[:, :, :HEAD_DIM].reshape(n, HEAD_DIM)
    v_ones = with_ones(kv_ref[:, :, HEAD_DIM : 2 * HEAD_DIM].reshape(n, HEAD_DIM))
    firsts = range(0, GROUP, count)
    scores = [scores_of(head_rows(q_ref, first, count), k) for first in firsts]
    for first, block in zip(firsts, scores):
        at = slice(first * rows, (first + count) * rows)
        largest, sums = weigh(block, v_ones)
        sums_ref[at, :] = sums
        largest_ref[at, :] = jnp.broadcast_to(largest, (count * rows, HEAD_DIM))


def far_kernel(count, completing_ref, mask_ref, q_ref, kv_ref, other_ref, sums_ref, largest_ref, out_ref):
    n = kv_ref.shape[0] * kv_ref.shape[1]
    blocks, rows_each = q_ref.shape[0], q_ref.shape[1]
    rows = blocks * rows_each
    core = lax.axis_index("core")
    section = lax.axis_index("half") * 2 + core
    finished = jnp.broadcast_to(completing_ref[...], mask_ref.shape)
    at_row = lax.broadcasted_iota(jnp.int32, mask_ref.shape, 0) == section
    at_column = lax.broadcasted_iota(jnp.int32, mask_ref.shape, 1) == finished
    visible = jnp.logical_and(mask_ref[...] == 1, section > finished)
    hit = jnp.logical_and(jnp.logical_and(at_row, at_column), visible)
    seen = jnp.max(jnp.where(hit, 1.0, 0.0)) > 0.5

    def store(first, total):
        out = total[:, :HEAD_DIM] / total[:, HEAD_DIM:]
        for i in range(count):
            g = first + i
            out_ref[:, :, g * HEAD_DIM : (g + 1) * HEAD_DIM] = (
                out[i * rows : (i + 1) * rows].astype(out_ref.dtype).reshape(blocks, rows_each, HEAD_DIM)
            )

    @pl.when(seen)
    def _():
        mine = kv_ref[:, :, 2 * HEAD_DIM :].reshape(n, HEAD_DIM)
        other = other_ref[...].reshape(n, HEAD_DIM)
        keys_here = core == 0
        k = jnp.where(keys_here, mine, other)
        v_ones = with_ones(jnp.where(keys_here, other, mine))
        firsts = range(0, GROUP, count)
        scores = [scores_of(head_rows(q_ref, first, count), k) for first in firsts]
        for first, block in zip(firsts, scores):
            at = slice(first * rows, (first + count) * rows)
            largest, sums = weigh(block, v_ones)
            before = largest_ref[at, :]
            after = jnp.maximum(before, largest)
            old = jnp.exp2((before - after) * BASE)
            new = jnp.exp2((largest - after) * BASE)
            old, new = jnp.concatenate([old, old], 1), jnp.concatenate([new, new], 1)
            store(first, sums_ref[at, :] * old + sums * new)

    @pl.when(jnp.logical_not(seen))
    def _():
        for first in range(0, GROUP, count):
            store(first, sums_ref[first * rows : (first + count) * rows, :])


def stage_kernel(query_ref, after_ref, keep_ref, send_ref, sems):
    del after_ref
    xb = lax.axis_index("xb")
    copies = []
    for z in range(KV_HEADS // 2):
        for i, (target, x) in enumerate(((keep_ref, xb), (send_ref, 1 - xb))):
            head = (z - FIRST_ZC) % 4 * 2 + x
            at = pl.ds(pl.multiple_of(head * WIDE, WIDE), WIDE)
            copies.append(pltpu.make_async_copy(query_ref.at[0, :, at], target.at[z], sems.at[2 * z + i]))
    for copy in copies:
        copy.start()
    for copy in copies:
        copy.wait()


def second_kernel(kept_ref, got_ref, keep_ref, send_ref):
    xb, low = lax.axis_index("xb"), lax.rem(lax.axis_index("zc"), 2)
    for source, x in ((kept_ref, xb), (got_ref, 1 - xb)):
        for high in range(2):
            keep_ref[x, high] = source[2 * high + low]
            send_ref[x, high] = source[2 * high + 1 - low]


def third_kernel(kept_ref, got_ref, keep_ref, send_ref):
    zc = lax.axis_index("zc")
    low, high = lax.rem(zc, 2), lax.div(zc, 2)
    for source, z in ((kept_ref, low), (got_ref, 1 - low)):
        for x in range(2):
            keep_ref[z, x] = source[x, high]
            send_ref[z, x] = source[x, 1 - high]


def last_kernel(kept_ref, got_ref, out_ref):
    high = lax.div(lax.axis_index("zc"), 2)
    for source, z in ((kept_ref, high), (got_ref, 1 - high)):
        for low in range(2):
            for x in range(2):
                place = lax.rem(2 * z + low + 4 - FIRST_ZC, 4)
                out_ref[2 * place + x] = source[low, x]


def pair_kernel(near_ref, sent_ref, after_ref, out_ref, late_ref):
    del after_ref
    late_ref[...] = sent_ref[...]
    for h in range(KV_HEADS):
        at = slice(h * HEAD_DIM, (h + 1) * HEAD_DIM)
        first = (h % 2) * 2 * HEAD_DIM
        for i in range(2):
            out_ref[h // 2, :, first + i * HEAD_DIM : first + (i + 1) * HEAD_DIM] = near_ref[i, :, at]


def pick_kernel(completing_ref, mine_ref, swapped_ref, out_ref):
    other = lax.bitwise_and(completing_ref[...], 1) != lax.axis_index("core")
    out_ref[...] = jnp.where(jnp.broadcast_to(other, out_ref.shape), swapped_ref[...], mine_ref[...])


def pack_keys_kernel(completing_ref, pairs_ref, picked_ref, late_ref, handed_ref, out_ref):
    upper = lax.axis_index("half") == 1
    handed = jnp.broadcast_to(jnp.where(upper, completing_ref[...], 2) < 2, handed_ref.shape)
    late = jnp.logical_and(upper, lax.axis_index("core") == 1)
    clean = jnp.where(handed, handed_ref[...], jnp.where(late, late_ref[...], picked_ref[...]))
    for h in range(KV_HEADS):
        first = (h % 2) * 3 * HEAD_DIM
        near = pairs_ref[h // 2, :, (h % 2) * 2 * HEAD_DIM : (h % 2 + 1) * 2 * HEAD_DIM]
        place = (h // 2 + FIRST_ZC) % 4
        for z in (place, place + 4):
            i = Z_ORDER.index(z)
            out_ref[i, :, first : first + 2 * HEAD_DIM] = near
            out_ref[i, :, first + 2 * HEAD_DIM : first + 3 * HEAD_DIM] = clean[:, h * HEAD_DIM : (h + 1) * HEAD_DIM]


def spread_kernel(served_ref, after_ref, out_ref):
    del after_ref
    rows = served_ref.shape[0] * served_ref.shape[1]
    each = 3 * HEAD_DIM
    for i in range(out_ref.shape[0]):
        head = (i // 4) % 2
        out_ref[i] = served_ref[:, :, head * each : (head + 1) * each].reshape(rows, each)


def clean_kernel(kv_ref, after_ref, out_ref):
    del after_ref
    out_ref[...] = kv_ref[:, :, 2 * HEAD_DIM :]


def estimate(q_rows, n):
    return pl.CostEstimate(flops=4 * q_rows * n * HEAD_DIM, bytes_accessed=4 * 2**20, transcendentals=q_rows * n)


def call(kernel, out_shape, specs, *operands, cost=None, mib=16):
    outs = (VMEM,) * len(out_shape) if isinstance(out_shape, tuple) else VMEM
    return pl.pallas_call(
        kernel,
        out_shape=out_shape,
        in_specs=specs,
        out_specs=outs,
        cost_estimate=cost,
        compiler_params=pltpu.CompilerParams(vmem_limit_bytes=mib * 2**20),
    )(*operands)


def shaped(*shape, dtype=jnp.bfloat16):
    return jax.ShapeDtypeStruct(shape, dtype)


def shards(query, key, value, clean_key, clean_value, completing, span_mask):
    tok = query.shape[1]
    heads = KV_HEADS
    z_all, served_by, plane_axes = ("zq", "zc"), ("zc", "xb"), ("xa", "xb", "y")
    depth, plane = 8, 16
    anywhere = pl.BlockSpec(memory_space=pl.ANY)

    width = heads * HEAD_DIM
    core = lax.axis_index("core")
    mine = jnp.where(core == 0, clean_key[0], clean_value[0])
    sent = jnp.where(core == 0, clean_value[0], clean_key[0])
    swapped = lax.ppermute(sent, ("half", "core"), [(0, 1), (1, 0)])
    finished = completing.reshape(1, 1)
    picked = call(pick_kernel, shaped(tok, width), [VMEM] * 3, finished, mine, swapped)
    handed = lax.ppermute(
        picked, ("half",) + z_all, [(z, depth + (z + depth // 2) % depth) for z in range(depth)]
    )
    near = jnp.stack([jnp.where(picked != picked, picked, a[0]) for a in (key, value)])
    pairs, late = call(
        pair_kernel,
        (shaped(heads // 2, tok, 4 * HEAD_DIM), shaped(tok, width)),
        [VMEM] * 2 + [anywhere],
        near,
        sent,
        picked,
    )
    late = lax.ppermute(late, ("half", "core"), [(2, 3)])

    kv = call(
        pack_keys_kernel,
        shaped(depth, tok, 6 * HEAD_DIM),
        [VMEM] * 5,
        finished,
        pairs,
        picked,
        late,
        handed,
    )
    part = heads // 2
    keep, send = pl.pallas_call(
        stage_kernel,
        out_shape=(shaped(part, tok, WIDE),) * 2,
        in_specs=[anywhere] * 2,
        out_specs=(VMEM,) * 2,
        scratch_shapes=[pltpu.SemaphoreType.DMA((heads,))],
        compiler_params=pltpu.CompilerParams(vmem_limit_bytes=16 * 2**20),
    )(query, kv)
    got = lax.ppermute(send, "xb", [(0, 1), (1, 0)])
    halves = (shaped(2, 2, tok, WIDE),) * 2
    keep, send = call(second_kernel, halves, [VMEM] * 2, keep, got)
    after_first = keep
    got = lax.ppermute(send, "zc", [(z, z ^ 1) for z in range(4)])
    keep, send = call(third_kernel, halves, [VMEM] * 2, keep, got)
    got = lax.ppermute(send, "zc", [(z, z ^ 2) for z in range(4)])
    served = call(last_kernel, shaped(heads, tok, WIDE), [VMEM] * 2, keep, got)


    kv = lax.all_to_all(kv, z_all, 0, 0, axis_index_groups=[Z_ORDER], tiled=True)
    kv = call(spread_kernel, shaped(plane, depth * tok, 3 * HEAD_DIM), [VMEM, anywhere], kv, after_first)
    kv = lax.all_to_all(kv, plane_axes, 0, 0, tiled=True)
    clean = call(clean_kernel, shaped(plane, depth * tok, HEAD_DIM), [VMEM, anywhere], kv, served)
    other = lax.ppermute(clean, "core", [(0, 1), (1, 0)])

    rows, n = heads * tok * GROUP, plane * depth * tok
    sums, largest = call(
        functools.partial(own_kernel, 3),
        (shaped(rows, 2 * HEAD_DIM, dtype=jnp.float32), shaped(rows, HEAD_DIM, dtype=jnp.float32)),
        [VMEM] * 2,
        served,
        kv,
        cost=estimate(rows, n),
        mib=40,
    )
    out = call(
        functools.partial(far_kernel, 3),
        shaped(heads, tok, WIDE),
        [VMEM] * 7,
        finished,
        span_mask,
        served,
        kv,
        other,
        sums,
        largest,
        cost=estimate(rows, n),
        mib=40,
    )
    out = lax.all_to_all(out, served_by, 0, 0, axis_index_groups=[SERVE_ORDER], tiled=True)
    return jnp.transpose(out, (1, 0, 2)).reshape(1, tok, HEADS * HEAD_DIM)


def solution(mesh):
    grid = Mesh(mesh.devices.reshape(2, 2, 2, 4, 2, 2, 4), ("half", "core", "zq", "zc", "xa", "xb", "y"))
    rows = P(("half", "core"), ("zq", "zc", "xa", "xb", "y"), None)
    return jax.shard_map(
        shards, mesh=grid, in_specs=(rows,) * 5 + (P(), P()), out_specs=rows, check_vma=False
    )
```

```python
import functools
import math

import jax
import jax.numpy as jnp
from jax import lax
from jax.experimental import pallas as pl
from jax.experimental.pallas import tpu as pltpu
from jax.sharding import Mesh
from jax.sharding import PartitionSpec as P

HEAD_DIM = 128
HEADS = 48
KV_HEADS = 8
GROUP = HEADS // KV_HEADS
WIDE = GROUP * HEAD_DIM
BASE = HEAD_DIM**-0.5 * math.log2(math.e)
Z_ORDER = [3, 4, 5, 6, 7, 0, 1, 2]
FIRST_ZC = 1
SERVE_ORDER = [(i + 2 * FIRST_ZC) % 8 for i in range(8)]
VMEM = pl.BlockSpec(memory_space=pltpu.VMEM)


def head_rows(q_ref, first, count):
    rows = q_ref.shape[0] * q_ref.shape[1]
    return jnp.concatenate(
        [
            q_ref[:, :, g * HEAD_DIM : (g + 1) * HEAD_DIM].reshape(rows, HEAD_DIM)
            for g in range(first, first + count)
        ],
        0,
    )


def scores_of(q, k):
    return lax.dot_general(q, k, (((1,), (1,)), ((), ())), preferred_element_type=jnp.float32)


def weigh(scores, v_ones):
    largest = jnp.max(scores, axis=-1, keepdims=True)
    weights = jnp.exp2((scores - largest) * BASE).astype(jnp.bfloat16)
    return largest, jnp.dot(weights, v_ones, preferred_element_type=jnp.float32)


def with_ones(v):
    return jnp.concatenate([v, jnp.ones_like(v)], 1)


def own_kernel(count, q_ref, kv_ref, sums_ref, largest_ref):
    n = kv_ref.shape[0] * kv_ref.shape[1]
    rows = q_ref.shape[0] * q_ref.shape[1]
    k = kv_ref[:, :, :HEAD_DIM].reshape(n, HEAD_DIM)
    v_ones = with_ones(kv_ref[:, :, HEAD_DIM : 2 * HEAD_DIM].reshape(n, HEAD_DIM))
    firsts = range(0, GROUP, count)
    scores = [scores_of(head_rows(q_ref, first, count), k) for first in firsts]
    for first, block in zip(firsts, scores):
        at = slice(first * rows, (first + count) * rows)
        largest, sums = weigh(block, v_ones)
        sums_ref[at, :] = sums
        largest_ref[at, :] = jnp.broadcast_to(largest, (count * rows, HEAD_DIM))


def alone_kernel(count, q_ref, kv_ref, out_ref):
    n = kv_ref.shape[0] * kv_ref.shape[1]
    blocks, rows_each = q_ref.shape[0], q_ref.shape[1]
    rows = blocks * rows_each
    k = kv_ref[:, :, :HEAD_DIM].reshape(n, HEAD_DIM)
    v_ones = with_ones(kv_ref[:, :, HEAD_DIM : 2 * HEAD_DIM].reshape(n, HEAD_DIM))
    firsts = range(0, GROUP, count)
    scores = [scores_of(head_rows(q_ref, first, count), k) for first in firsts]
    for first, block in zip(firsts, scores):
        largest, sums = weigh(block, v_ones)
        out = sums[:, :HEAD_DIM] / sums[:, HEAD_DIM:]
        for i in range(count):
            g = first + i
            out_ref[:, :, g * HEAD_DIM : (g + 1) * HEAD_DIM] = (
                out[i * rows : (i + 1) * rows].astype(out_ref.dtype).reshape(blocks, rows_each, HEAD_DIM)
            )


def far_kernel(count, completing_ref, mask_ref, q_ref, kv_ref, other_ref, sums_ref, largest_ref, out_ref):
    n = kv_ref.shape[0] * kv_ref.shape[1]
    blocks, rows_each = q_ref.shape[0], q_ref.shape[1]
    rows = blocks * rows_each
    core = lax.axis_index("core")
    section = lax.axis_index("half") * 2 + core
    finished = jnp.broadcast_to(completing_ref[...], mask_ref.shape)
    at_row = lax.broadcasted_iota(jnp.int32, mask_ref.shape, 0) == section
    at_column = lax.broadcasted_iota(jnp.int32, mask_ref.shape, 1) == finished
    visible = jnp.logical_and(mask_ref[...] == 1, section > finished)
    hit = jnp.logical_and(jnp.logical_and(at_row, at_column), visible)
    seen = jnp.max(jnp.where(hit, 1.0, 0.0)) > 0.5

    def store(first, total):
        out = total[:, :HEAD_DIM] / total[:, HEAD_DIM:]
        for i in range(count):
            g = first + i
            out_ref[:, :, g * HEAD_DIM : (g + 1) * HEAD_DIM] = (
                out[i * rows : (i + 1) * rows].astype(out_ref.dtype).reshape(blocks, rows_each, HEAD_DIM)
            )

    @pl.when(seen)
    def _():
        mine = kv_ref[:, :, 2 * HEAD_DIM :].reshape(n, HEAD_DIM)
        other = other_ref[...].reshape(n, HEAD_DIM)
        keys_here = core == 0
        k = jnp.where(keys_here, mine, other)
        v_ones = with_ones(jnp.where(keys_here, other, mine))
        firsts = range(0, GROUP, count)
        scores = [scores_of(head_rows(q_ref, first, count), k) for first in firsts]
        for first, block in zip(firsts, scores):
            at = slice(first * rows, (first + count) * rows)
            largest, sums = weigh(block, v_ones)
            before = largest_ref[at, :]
            after = jnp.maximum(before, largest)
            old = jnp.exp2((before - after) * BASE)
            new = jnp.exp2((largest - after) * BASE)
            old, new = jnp.concatenate([old, old], 1), jnp.concatenate([new, new], 1)
            store(first, sums_ref[at, :] * old + sums * new)

    @pl.when(jnp.logical_not(seen))
    def _():
        for first in range(0, GROUP, count):
            store(first, sums_ref[first * rows : (first + count) * rows, :])


def stage_kernel(query_ref, after_ref, keep_ref, send_ref, sems):
    del after_ref
    xb = lax.axis_index("xb")
    copies = []
    for z in range(KV_HEADS // 2):
        for i, (target, x) in enumerate(((keep_ref, xb), (send_ref, 1 - xb))):
            head = (z - FIRST_ZC) % 4 * 2 + x
            at = pl.ds(pl.multiple_of(head * WIDE, WIDE), WIDE)
            copies.append(pltpu.make_async_copy(query_ref.at[0, :, at], target.at[z], sems.at[2 * z + i]))
    for copy in copies:
        copy.start()
    for copy in copies:
        copy.wait()


def second_kernel(kept_ref, got_ref, keep_ref, send_ref):
    xb, low = lax.axis_index("xb"), lax.rem(lax.axis_index("zc"), 2)
    for source, x in ((kept_ref, xb), (got_ref, 1 - xb)):
        for high in range(2):
            keep_ref[x, high] = source[2 * high + low]
            send_ref[x, high] = source[2 * high + 1 - low]


def third_kernel(kept_ref, got_ref, keep_ref, send_ref):
    zc = lax.axis_index("zc")
    low, high = lax.rem(zc, 2), lax.div(zc, 2)
    for source, z in ((kept_ref, low), (got_ref, 1 - low)):
        for x in range(2):
            keep_ref[z, x] = source[x, high]
            send_ref[z, x] = source[x, 1 - high]


def last_kernel(kept_ref, got_ref, out_ref):
    high = lax.div(lax.axis_index("zc"), 2)
    for source, z in ((kept_ref, high), (got_ref, 1 - high)):
        for low in range(2):
            for x in range(2):
                place = lax.rem(2 * z + low + 4 - FIRST_ZC, 4)
                out_ref[2 * place + x] = source[low, x]


def pair_kernel(near_ref, sent_ref, after_ref, out_ref, late_ref):
    del after_ref
    late_ref[...] = sent_ref[...]
    for h in range(KV_HEADS):
        at = slice(h * HEAD_DIM, (h + 1) * HEAD_DIM)
        first = (h % 2) * 2 * HEAD_DIM
        for i in range(2):
            out_ref[h // 2, :, first + i * HEAD_DIM : first + (i + 1) * HEAD_DIM] = near_ref[i, :, at]


def pick_kernel(completing_ref, mine_ref, swapped_ref, out_ref):
    other = lax.bitwise_and(completing_ref[...], 1) != lax.axis_index("core")
    out_ref[...] = jnp.where(jnp.broadcast_to(other, out_ref.shape), swapped_ref[...], mine_ref[...])


def pack_keys_kernel(completing_ref, pairs_ref, picked_ref, late_ref, handed_ref, out_ref):
    upper = lax.axis_index("half") == 1
    handed = jnp.broadcast_to(jnp.where(upper, completing_ref[...], 2) < 2, handed_ref.shape)
    late = jnp.logical_and(upper, lax.axis_index("core") == 1)
    clean = jnp.where(handed, handed_ref[...], jnp.where(late, late_ref[...], picked_ref[...]))
    for h in range(KV_HEADS):
        first = (h % 2) * 3 * HEAD_DIM
        near = pairs_ref[h // 2, :, (h % 2) * 2 * HEAD_DIM : (h % 2 + 1) * 2 * HEAD_DIM]
        place = (h // 2 + FIRST_ZC) % 4
        for z in (place, place + 4):
            i = Z_ORDER.index(z)
            out_ref[i, :, first : first + 2 * HEAD_DIM] = near
            out_ref[i, :, first + 2 * HEAD_DIM : first + 3 * HEAD_DIM] = clean[:, h * HEAD_DIM : (h + 1) * HEAD_DIM]


def spread_kernel(served_ref, after_ref, out_ref):
    del after_ref
    rows = served_ref.shape[0] * served_ref.shape[1]
    each = 3 * HEAD_DIM
    width = out_ref.shape[2]
    for i in range(out_ref.shape[0]):
        head = (i // 4) % 2
        out_ref[i] = served_ref[:, :, head * each : head * each + width].reshape(rows, width)


def clean_kernel(kv_ref, after_ref, out_ref):
    del after_ref
    out_ref[...] = kv_ref[:, :, 2 * HEAD_DIM :]


def estimate(q_rows, n):
    return pl.CostEstimate(flops=4 * q_rows * n * HEAD_DIM, bytes_accessed=4 * 2**20, transcendentals=q_rows * n)


def call(kernel, out_shape, specs, *operands, cost=None, mib=16):
    outs = (VMEM,) * len(out_shape) if isinstance(out_shape, tuple) else VMEM
    return pl.pallas_call(
        kernel,
        out_shape=out_shape,
        in_specs=specs,
        out_specs=outs,
        cost_estimate=cost,
        compiler_params=pltpu.CompilerParams(vmem_limit_bytes=mib * 2**20),
    )(*operands)


def shaped(*shape, dtype=jnp.bfloat16):
    return jax.ShapeDtypeStruct(shape, dtype)


def shards(query, key, value, clean_key, clean_value, completing, span_mask):
    tok = query.shape[1]
    heads = KV_HEADS
    z_all, served_by, plane_axes = ("zq", "zc"), ("zc", "xb"), ("xa", "xb", "y")
    depth, plane = 8, 16
    anywhere = pl.BlockSpec(memory_space=pl.ANY)

    width = heads * HEAD_DIM
    core = lax.axis_index("core")
    mine = jnp.where(core == 0, clean_key[0], clean_value[0])
    sent = jnp.where(core == 0, clean_value[0], clean_key[0])
    swapped = lax.ppermute(sent, ("half", "core"), [(0, 1), (1, 0)])
    finished = completing.reshape(1, 1)
    picked = call(pick_kernel, shaped(tok, width), [VMEM] * 3, finished, mine, swapped)
    handed = lax.ppermute(
        picked, ("half",) + z_all, [(z, depth + (z + depth // 2) % depth) for z in range(depth)]
    )
    near = jnp.stack([jnp.where(picked != picked, picked, a[0]) for a in (key, value)])
    pairs, late = call(
        pair_kernel,
        (shaped(heads // 2, tok, 4 * HEAD_DIM), shaped(tok, width)),
        [VMEM] * 2 + [anywhere],
        near,
        sent,
        picked,
    )
    late = lax.ppermute(late, ("half", "core"), [(2, 3)])

    kv = call(
        pack_keys_kernel,
        shaped(depth, tok, 6 * HEAD_DIM),
        [VMEM] * 5,
        finished,
        pairs,
        picked,
        late,
        handed,
    )
    part = heads // 2
    keep, send = pl.pallas_call(
        stage_kernel,
        out_shape=(shaped(part, tok, WIDE),) * 2,
        in_specs=[anywhere] * 2,
        out_specs=(VMEM,) * 2,
        scratch_shapes=[pltpu.SemaphoreType.DMA((heads,))],
        compiler_params=pltpu.CompilerParams(vmem_limit_bytes=16 * 2**20),
    )(query, kv)
    got = lax.ppermute(send, "xb", [(0, 1), (1, 0)])
    halves = (shaped(2, 2, tok, WIDE),) * 2
    keep, send = call(second_kernel, halves, [VMEM] * 2, keep, got)
    kv = lax.all_to_all(kv, z_all, 0, 0, axis_index_groups=[Z_ORDER], tiled=True)
    rows, n = heads * tok * GROUP, plane * depth * tok

    def gather(kv, keep, send, width):
        own = call(spread_kernel, shaped(plane, depth * tok, width), [VMEM, anywhere], kv, keep)
        own = lax.all_to_all(own, plane_axes, 0, 0, tiled=True)
        got = lax.ppermute(send, "zc", [(z, z ^ 1) for z in range(4)])
        keep, send = call(third_kernel, halves, [VMEM] * 2, keep, got)
        got = lax.ppermute(send, "zc", [(z, z ^ 2) for z in range(4)])
        return own, call(last_kernel, shaped(heads, tok, WIDE), [VMEM] * 2, keep, got)

    def with_clean(kv, keep, send, finished, span_mask):
        kv, served = gather(kv, keep, send, 3 * HEAD_DIM)
        clean = call(clean_kernel, shaped(plane, depth * tok, HEAD_DIM), [VMEM, anywhere], kv, served)
        other = lax.ppermute(clean, "core", [(0, 1), (1, 0)])
        sums, largest = call(
            functools.partial(own_kernel, 3),
            (shaped(rows, 2 * HEAD_DIM, dtype=jnp.float32), shaped(rows, HEAD_DIM, dtype=jnp.float32)),
            [VMEM] * 2,
            served,
            kv,
            cost=estimate(rows, n),
            mib=40,
        )
        return call(
            functools.partial(far_kernel, 3),
            shaped(heads, tok, WIDE),
            [VMEM] * 7,
            finished,
            span_mask,
            served,
            kv,
            other,
            sums,
            largest,
            cost=estimate(rows, n),
            mib=40,
        )

    def without(kv, keep, send, finished, span_mask):
        kv, served = gather(kv, keep, send, 2 * HEAD_DIM)
        return call(
            functools.partial(alone_kernel, 3),
            shaped(heads, tok, WIDE),
            [VMEM] * 2,
            served,
            kv,
            cost=estimate(rows, n),
            mib=40,
        )

    may_see = 2 * lax.axis_index("half") + 1 > completing[0]
    out = lax.cond(may_see, with_clean, without, kv, keep, send, finished, span_mask)
    out = lax.all_to_all(out, served_by, 0, 0, axis_index_groups=[SERVE_ORDER], tiled=True)
    return jnp.transpose(out, (1, 0, 2)).reshape(1, tok, HEADS * HEAD_DIM)


def solution(mesh):
    grid = Mesh(mesh.devices.reshape(2, 2, 2, 4, 2, 2, 4), ("half", "core", "zq", "zc", "xa", "xb", "y"))
    rows = P(("half", "core"), ("zq", "zc", "xa", "xb", "y"), None)
    return jax.shard_map(
        shards, mesh=grid, in_specs=(rows,) * 5 + (P(), P()), out_specs=rows, check_vma=False
    )
```

```python
import functools
import math

import jax
import jax.numpy as jnp
from jax import lax
from jax.experimental import pallas as pl
from jax.experimental.pallas import tpu as pltpu
from jax.sharding import Mesh
from jax.sharding import PartitionSpec as P

HEAD_DIM = 128
HEADS = 48
KV_HEADS = 8
GROUP = HEADS // KV_HEADS
WIDE = GROUP * HEAD_DIM
BASE = HEAD_DIM**-0.5 * math.log2(math.e)
Z_ORDER = [3, 4, 5, 6, 7, 0, 1, 2]
FIRST_ZC = 1
SERVE_ORDER = [(i + 2 * FIRST_ZC) % 8 for i in range(8)]
VMEM = pl.BlockSpec(memory_space=pltpu.VMEM)


def head_rows(q_ref, first, count):
    rows = q_ref.shape[0] * q_ref.shape[1]
    return jnp.concatenate(
        [
            q_ref[:, :, g * HEAD_DIM : (g + 1) * HEAD_DIM].reshape(rows, HEAD_DIM)
            for g in range(first, first + count)
        ],
        0,
    )


def scores_of(q, k):
    return lax.dot_general(q, k, (((1,), (1,)), ((), ())), preferred_element_type=jnp.float32)


def weigh(scores, v_ones):
    largest = jnp.max(scores, axis=-1, keepdims=True)
    weights = jnp.exp2((scores - largest) * BASE).astype(jnp.bfloat16)
    return largest, jnp.dot(weights, v_ones, preferred_element_type=jnp.float32)


def with_ones(v):
    return jnp.concatenate([v, jnp.ones_like(v)], 1)


def own_kernel(count, q_ref, kv_ref, sums_ref, largest_ref):
    n = kv_ref.shape[0] * kv_ref.shape[1]
    rows = q_ref.shape[0] * q_ref.shape[1]
    k = kv_ref[:, :, :HEAD_DIM].reshape(n, HEAD_DIM)
    v_ones = with_ones(kv_ref[:, :, HEAD_DIM : 2 * HEAD_DIM].reshape(n, HEAD_DIM))
    firsts = range(0, GROUP, count)
    scores = [scores_of(head_rows(q_ref, first, count), k) for first in firsts]
    for first, block in zip(firsts, scores):
        at = slice(first * rows, (first + count) * rows)
        largest, sums = weigh(block, v_ones)
        sums_ref[at, :] = sums
        largest_ref[at, :] = jnp.broadcast_to(largest, (count * rows, HEAD_DIM))


def alone_kernel(count, q_ref, kv_ref, out_ref):
    n = kv_ref.shape[0] * kv_ref.shape[1]
    blocks, rows_each = q_ref.shape[0], q_ref.shape[1]
    rows = blocks * rows_each
    k = kv_ref[:, :, :HEAD_DIM].reshape(n, HEAD_DIM)
    v_ones = with_ones(kv_ref[:, :, HEAD_DIM : 2 * HEAD_DIM].reshape(n, HEAD_DIM))
    firsts = range(0, GROUP, count)
    scores = [scores_of(head_rows(q_ref, first, count), k) for first in firsts]
    for first, block in zip(firsts, scores):
        largest, sums = weigh(block, v_ones)
        out = sums[:, :HEAD_DIM] / sums[:, HEAD_DIM:]
        for i in range(count):
            g = first + i
            out_ref[:, :, g * HEAD_DIM : (g + 1) * HEAD_DIM] = (
                out[i * rows : (i + 1) * rows].astype(out_ref.dtype).reshape(blocks, rows_each, HEAD_DIM)
            )


def far_kernel(count, completing_ref, mask_ref, q_ref, kv_ref, other_ref, sums_ref, largest_ref, out_ref):
    n = kv_ref.shape[0] * kv_ref.shape[1]
    blocks, rows_each = q_ref.shape[0], q_ref.shape[1]
    rows = blocks * rows_each
    core = lax.axis_index("core")
    section = lax.axis_index("half") * 2 + core
    finished = jnp.broadcast_to(completing_ref[...], mask_ref.shape)
    at_row = lax.broadcasted_iota(jnp.int32, mask_ref.shape, 0) == section
    at_column = lax.broadcasted_iota(jnp.int32, mask_ref.shape, 1) == finished
    visible = jnp.logical_and(mask_ref[...] == 1, section > finished)
    hit = jnp.logical_and(jnp.logical_and(at_row, at_column), visible)
    seen = jnp.max(jnp.where(hit, 1.0, 0.0)) > 0.5

    def store(first, total):
        out = total[:, :HEAD_DIM] / total[:, HEAD_DIM:]
        for i in range(count):
            g = first + i
            out_ref[:, :, g * HEAD_DIM : (g + 1) * HEAD_DIM] = (
                out[i * rows : (i + 1) * rows].astype(out_ref.dtype).reshape(blocks, rows_each, HEAD_DIM)
            )

    @pl.when(seen)
    def _():
        mine = kv_ref[:, :, 2 * HEAD_DIM :].reshape(n, HEAD_DIM)
        other = other_ref[...].reshape(n, HEAD_DIM)
        keys_here = core == 0
        k = jnp.where(keys_here, mine, other)
        v_ones = with_ones(jnp.where(keys_here, other, mine))
        firsts = range(0, GROUP, count)
        scores = [scores_of(head_rows(q_ref, first, count), k) for first in firsts]
        for first, block in zip(firsts, scores):
            at = slice(first * rows, (first + count) * rows)
            largest, sums = weigh(block, v_ones)
            before = largest_ref[at, :]
            after = jnp.maximum(before, largest)
            old = jnp.exp2((before - after) * BASE)
            new = jnp.exp2((largest - after) * BASE)
            old, new = jnp.concatenate([old, old], 1), jnp.concatenate([new, new], 1)
            store(first, sums_ref[at, :] * old + sums * new)

    @pl.when(jnp.logical_not(seen))
    def _():
        for first in range(0, GROUP, count):
            store(first, sums_ref[first * rows : (first + count) * rows, :])


def stage_kernel(query_ref, after_ref, keep_ref, send_ref, sems):
    del after_ref
    xb = lax.axis_index("xb")
    copies = []
    for z in range(KV_HEADS // 2):
        for i, (target, x) in enumerate(((keep_ref, xb), (send_ref, 1 - xb))):
            head = (z - FIRST_ZC) % 4 * 2 + x
            at = pl.ds(pl.multiple_of(head * WIDE, WIDE), WIDE)
            copies.append(pltpu.make_async_copy(query_ref.at[0, :, at], target.at[z], sems.at[2 * z + i]))
    for copy in copies:
        copy.start()
    for copy in copies:
        copy.wait()


def second_kernel(kept_ref, got_ref, keep_ref, send_ref):
    xb, low = lax.axis_index("xb"), lax.rem(lax.axis_index("zc"), 2)
    for source, x in ((kept_ref, xb), (got_ref, 1 - xb)):
        for high in range(2):
            keep_ref[x, high] = source[2 * high + low]
            send_ref[x, high] = source[2 * high + 1 - low]


def third_kernel(kept_ref, got_ref, keep_ref, send_ref):
    zc = lax.axis_index("zc")
    low, high = lax.rem(zc, 2), lax.div(zc, 2)
    for source, z in ((kept_ref, low), (got_ref, 1 - low)):
        for x in range(2):
            keep_ref[z, x] = source[x, high]
            send_ref[z, x] = source[x, 1 - high]


def last_kernel(kept_ref, got_ref, out_ref):
    high = lax.div(lax.axis_index("zc"), 2)
    for source, z in ((kept_ref, high), (got_ref, 1 - high)):
        for low in range(2):
            for x in range(2):
                place = lax.rem(2 * z + low + 4 - FIRST_ZC, 4)
                out_ref[2 * place + x] = source[low, x]


def pair_kernel(near_ref, after_ref, out_ref):
    del after_ref
    for h in range(KV_HEADS):
        at = slice(h * HEAD_DIM, (h + 1) * HEAD_DIM)
        first = (h % 2) * 2 * HEAD_DIM
        for i in range(2):
            out_ref[h // 2, :, first + i * HEAD_DIM : first + (i + 1) * HEAD_DIM] = near_ref[i, :, at]


def pick_kernel(completing_ref, mine_ref, swapped_ref, out_ref):
    other = lax.bitwise_and(completing_ref[...], 1) != lax.axis_index("core")
    out_ref[...] = jnp.where(jnp.broadcast_to(other, out_ref.shape), swapped_ref[...], mine_ref[...])


def pack_keys_kernel(axis, pairs_ref, mine_ref, got_ref, out_ref):
    clean = jnp.where(lax.axis_index(axis) == 1, got_ref[...], mine_ref[...])
    for h in range(KV_HEADS):
        first = (h % 2) * 3 * HEAD_DIM
        near = pairs_ref[h // 2, :, (h % 2) * 2 * HEAD_DIM : (h % 2 + 1) * 2 * HEAD_DIM]
        place = (h // 2 + FIRST_ZC) % 4
        for z in (place, place + 4):
            i = Z_ORDER.index(z)
            out_ref[i, :, first : first + 2 * HEAD_DIM] = near
            out_ref[i, :, first + 2 * HEAD_DIM : first + 3 * HEAD_DIM] = clean[:, h * HEAD_DIM : (h + 1) * HEAD_DIM]


def spread_kernel(served_ref, after_ref, out_ref):
    del after_ref
    rows = served_ref.shape[0] * served_ref.shape[1]
    each = 3 * HEAD_DIM
    width = out_ref.shape[2]
    for i in range(out_ref.shape[0]):
        head = (i // 4) % 2
        out_ref[i] = served_ref[:, :, head * each : head * each + width].reshape(rows, width)


def clean_kernel(kv_ref, after_ref, out_ref):
    del after_ref
    out_ref[...] = kv_ref[:, :, 2 * HEAD_DIM :]


def estimate(q_rows, n):
    return pl.CostEstimate(flops=4 * q_rows * n * HEAD_DIM, bytes_accessed=4 * 2**20, transcendentals=q_rows * n)


def call(kernel, out_shape, specs, *operands, cost=None, mib=16):
    outs = (VMEM,) * len(out_shape) if isinstance(out_shape, tuple) else VMEM
    return pl.pallas_call(
        kernel,
        out_shape=out_shape,
        in_specs=specs,
        out_specs=outs,
        cost_estimate=cost,
        compiler_params=pltpu.CompilerParams(vmem_limit_bytes=mib * 2**20),
    )(*operands)


def shaped(*shape, dtype=jnp.bfloat16):
    return jax.ShapeDtypeStruct(shape, dtype)


def shards(query, key, value, clean_key, clean_value, completing, span_mask):
    tok = query.shape[1]
    heads = KV_HEADS
    z_all, served_by, plane_axes = ("zq", "zc"), ("zc", "xb"), ("xa", "xb", "y")
    depth, plane = 8, 16
    anywhere = pl.BlockSpec(memory_space=pl.ANY)

    width = heads * HEAD_DIM
    finished = completing.reshape(1, 1)
    core = lax.axis_index("core")

    def packed(axis, near, mine, got):
        near = call(pair_kernel, shaped(heads // 2, tok, 4 * HEAD_DIM), [VMEM, anywhere], near, mine)
        return call(
            functools.partial(pack_keys_kernel, axis), shaped(depth, tok, 6 * HEAD_DIM), [VMEM] * 3, near, mine, got
        )

    def handed_over(key, value, clean_key, clean_value, finished):
        mine = jnp.where(core == 0, clean_key[0], clean_value[0])
        sent = jnp.where(core == 0, clean_value[0], clean_key[0])
        swapped = lax.ppermute(sent, ("half", "core"), [(0, 1), (1, 0)])
        picked = call(pick_kernel, shaped(tok, width), [VMEM] * 3, finished, mine, swapped)
        handed = lax.ppermute(
            picked, ("half",) + z_all, [(z, depth + (z + depth // 2) % depth) for z in range(depth)]
        )
        near = jnp.stack([jnp.where(picked != picked, picked, a[0]) for a in (key, value)])
        return packed("half", near, picked, handed)

    def kept(key, value, clean_key, clean_value, finished):
        del finished
        mine = jnp.where(core == 0, clean_key[0], clean_value[0])
        got = lax.ppermute(clean_value[0], ("half", "core"), [(2, 3)])
        return packed("core", jnp.stack([key[0], value[0]]), mine, got)

    kv = lax.cond(completing[0] < 2, handed_over, kept, key, value, clean_key, clean_value, finished)
    part = heads // 2
    keep, send = pl.pallas_call(
        stage_kernel,
        out_shape=(shaped(part, tok, WIDE),) * 2,
        in_specs=[anywhere] * 2,
        out_specs=(VMEM,) * 2,
        scratch_shapes=[pltpu.SemaphoreType.DMA((heads,))],
        compiler_params=pltpu.CompilerParams(vmem_limit_bytes=16 * 2**20),
    )(query, kv)
    got = lax.ppermute(send, "xb", [(0, 1), (1, 0)])
    halves = (shaped(2, 2, tok, WIDE),) * 2
    keep, send = call(second_kernel, halves, [VMEM] * 2, keep, got)
    kv = lax.all_to_all(kv, z_all, 0, 0, axis_index_groups=[Z_ORDER], tiled=True)
    rows, n = heads * tok * GROUP, plane * depth * tok

    def gather(kv, keep, send, width):
        own = call(spread_kernel, shaped(plane, depth * tok, width), [VMEM, anywhere], kv, keep)
        own = lax.all_to_all(own, plane_axes, 0, 0, tiled=True)
        got = lax.ppermute(send, "zc", [(z, z ^ 1) for z in range(4)])
        keep, send = call(third_kernel, halves, [VMEM] * 2, keep, got)
        got = lax.ppermute(send, "zc", [(z, z ^ 2) for z in range(4)])
        return own, call(last_kernel, shaped(heads, tok, WIDE), [VMEM] * 2, keep, got)

    def with_clean(kv, keep, send, finished, span_mask):
        kv, served = gather(kv, keep, send, 3 * HEAD_DIM)
        clean = call(clean_kernel, shaped(plane, depth * tok, HEAD_DIM), [VMEM, anywhere], kv, served)
        other = lax.ppermute(clean, "core", [(0, 1), (1, 0)])
        sums, largest = call(
            functools.partial(own_kernel, 3),
            (shaped(rows, 2 * HEAD_DIM, dtype=jnp.float32), shaped(rows, HEAD_DIM, dtype=jnp.float32)),
            [VMEM] * 2,
            served,
            kv,
            cost=estimate(rows, n),
            mib=40,
        )
        return call(
            functools.partial(far_kernel, 3),
            shaped(heads, tok, WIDE),
            [VMEM] * 7,
            finished,
            span_mask,
            served,
            kv,
            other,
            sums,
            largest,
            cost=estimate(rows, n),
            mib=40,
        )

    def without(kv, keep, send, finished, span_mask):
        kv, served = gather(kv, keep, send, 2 * HEAD_DIM)
        return call(
            functools.partial(alone_kernel, 3),
            shaped(heads, tok, WIDE),
            [VMEM] * 2,
            served,
            kv,
            cost=estimate(rows, n),
            mib=40,
        )

    may_see = 2 * lax.axis_index("half") + 1 > completing[0]
    out = lax.cond(may_see, with_clean, without, kv, keep, send, finished, span_mask)
    out = lax.all_to_all(out, served_by, 0, 0, axis_index_groups=[SERVE_ORDER], tiled=True)
    return jnp.transpose(out, (1, 0, 2)).reshape(1, tok, HEADS * HEAD_DIM)


def solution(mesh):
    grid = Mesh(mesh.devices.reshape(2, 2, 2, 4, 2, 2, 4), ("half", "core", "zq", "zc", "xa", "xb", "y"))
    rows = P(("half", "core"), ("zq", "zc", "xa", "xb", "y"), None)
    return jax.shard_map(
        shards, mesh=grid, in_specs=(rows,) * 5 + (P(), P()), out_specs=rows, check_vma=False
    )
```

```python
import functools
import math

import jax
import jax.numpy as jnp
from jax import lax
from jax.experimental import pallas as pl
from jax.experimental.pallas import tpu as pltpu
from jax.sharding import Mesh
from jax.sharding import PartitionSpec as P

HEAD_DIM = 128
HEADS = 48
KV_HEADS = 8
GROUP = HEADS // KV_HEADS
WIDE = GROUP * HEAD_DIM
BASE = HEAD_DIM**-0.5 * math.log2(math.e)
Z_ORDER = [3, 4, 5, 6, 7, 0, 1, 2]
FIRST_ZC = 1
SERVE_ORDER = [(i + 2 * FIRST_ZC) % 8 for i in range(8)]
VMEM = pl.BlockSpec(memory_space=pltpu.VMEM)


def head_rows(q_ref, first, count):
    rows = q_ref.shape[0] * q_ref.shape[1]
    return jnp.concatenate(
        [
            q_ref[:, :, g * HEAD_DIM : (g + 1) * HEAD_DIM].reshape(rows, HEAD_DIM)
            for g in range(first, first + count)
        ],
        0,
    )


def scores_of(q, k):
    return lax.dot_general(q, k, (((1,), (1,)), ((), ())), preferred_element_type=jnp.float32)


def weigh(scores, v_ones):
    largest = jnp.max(scores, axis=-1, keepdims=True)
    weights = jnp.exp2((scores - largest) * BASE).astype(jnp.bfloat16)
    return largest, jnp.dot(weights, v_ones, preferred_element_type=jnp.float32)


def with_ones(v):
    return jnp.concatenate([v, jnp.ones_like(v)], 1)


def own_kernel(count, q_ref, kv_ref, sums_ref, largest_ref):
    n = kv_ref.shape[0] * kv_ref.shape[1]
    rows = q_ref.shape[0] * q_ref.shape[1]
    k = kv_ref[:, :, :HEAD_DIM].reshape(n, HEAD_DIM)
    v_ones = with_ones(kv_ref[:, :, HEAD_DIM : 2 * HEAD_DIM].reshape(n, HEAD_DIM))
    firsts = range(0, GROUP, count)
    scores = [scores_of(head_rows(q_ref, first, count), k) for first in firsts]
    for first, block in zip(firsts, scores):
        at = slice(first * rows, (first + count) * rows)
        largest, sums = weigh(block, v_ones)
        sums_ref[at, :] = sums
        largest_ref[at, :] = jnp.broadcast_to(largest, (count * rows, HEAD_DIM))


def alone_kernel(count, q_ref, kv_ref, out_ref):
    n = kv_ref.shape[0] * kv_ref.shape[1]
    blocks, rows_each = q_ref.shape[0], q_ref.shape[1]
    rows = blocks * rows_each
    k = kv_ref[:, :, :HEAD_DIM].reshape(n, HEAD_DIM)
    v_ones = with_ones(kv_ref[:, :, HEAD_DIM : 2 * HEAD_DIM].reshape(n, HEAD_DIM))
    firsts = range(0, GROUP, count)
    scores = [scores_of(head_rows(q_ref, first, count), k) for first in firsts]
    for first, block in zip(firsts, scores):
        largest, sums = weigh(block, v_ones)
        out = sums[:, :HEAD_DIM] / sums[:, HEAD_DIM:]
        for i in range(count):
            g = first + i
            out_ref[:, :, g * HEAD_DIM : (g + 1) * HEAD_DIM] = (
                out[i * rows : (i + 1) * rows].astype(out_ref.dtype).reshape(blocks, rows_each, HEAD_DIM)
            )


def far_kernel(count, completing_ref, mask_ref, q_ref, kv_ref, other_ref, sums_ref, largest_ref, out_ref):
    n = kv_ref.shape[0] * kv_ref.shape[1]
    blocks, rows_each = q_ref.shape[0], q_ref.shape[1]
    rows = blocks * rows_each
    core = lax.axis_index("core")
    section = lax.axis_index("half") * 2 + core
    finished = jnp.broadcast_to(completing_ref[...], mask_ref.shape)
    at_row = lax.broadcasted_iota(jnp.int32, mask_ref.shape, 0) == section
    at_column = lax.broadcasted_iota(jnp.int32, mask_ref.shape, 1) == finished
    visible = jnp.logical_and(mask_ref[...] == 1, section > finished)
    hit = jnp.logical_and(jnp.logical_and(at_row, at_column), visible)
    seen = jnp.max(jnp.where(hit, 1.0, 0.0)) > 0.5

    def store(first, total):
        out = total[:, :HEAD_DIM] / total[:, HEAD_DIM:]
        for i in range(count):
            g = first + i
            out_ref[:, :, g * HEAD_DIM : (g + 1) * HEAD_DIM] = (
                out[i * rows : (i + 1) * rows].astype(out_ref.dtype).reshape(blocks, rows_each, HEAD_DIM)
            )

    @pl.when(seen)
    def _():
        mine = kv_ref[:, :, 2 * HEAD_DIM :].reshape(n, HEAD_DIM)
        other = other_ref[...].reshape(n, HEAD_DIM)
        keys_here = core == 0
        k = jnp.where(keys_here, mine, other)
        v_ones = with_ones(jnp.where(keys_here, other, mine))
        firsts = range(0, GROUP, count)
        scores = [scores_of(head_rows(q_ref, first, count), k) for first in firsts]
        for first, block in zip(firsts, scores):
            at = slice(first * rows, (first + count) * rows)
            largest, sums = weigh(block, v_ones)
            before = largest_ref[at, :]
            after = jnp.maximum(before, largest)
            old = jnp.exp2((before - after) * BASE)
            new = jnp.exp2((largest - after) * BASE)
            old, new = jnp.concatenate([old, old], 1), jnp.concatenate([new, new], 1)
            store(first, sums_ref[at, :] * old + sums * new)

    @pl.when(jnp.logical_not(seen))
    def _():
        for first in range(0, GROUP, count):
            store(first, sums_ref[first * rows : (first + count) * rows, :])


def stage_kernel(query_ref, after_ref, keep_ref, send_ref, sems):
    del after_ref
    xb = lax.axis_index("xb")
    copies = []
    for z in range(KV_HEADS // 2):
        for i, (target, x) in enumerate(((keep_ref, xb), (send_ref, 1 - xb))):
            head = (z - FIRST_ZC) % 4 * 2 + x
            at = pl.ds(pl.multiple_of(head * WIDE, WIDE), WIDE)
            copies.append(pltpu.make_async_copy(query_ref.at[0, :, at], target.at[z], sems.at[2 * z + i]))
    for copy in copies:
        copy.start()
    for copy in copies:
        copy.wait()


def second_kernel(kept_ref, got_ref, keep_ref, send_ref):
    xb, low = lax.axis_index("xb"), lax.rem(lax.axis_index("zc"), 2)
    for source, x in ((kept_ref, xb), (got_ref, 1 - xb)):
        for high in range(2):
            keep_ref[x, high] = source[2 * high + low]
            send_ref[x, high] = source[2 * high + 1 - low]


def third_kernel(kept_ref, got_ref, keep_ref, send_ref):
    zc = lax.axis_index("zc")
    low, high = lax.rem(zc, 2), lax.div(zc, 2)
    for source, z in ((kept_ref, low), (got_ref, 1 - low)):
        for x in range(2):
            keep_ref[z, x] = source[x, high]
            send_ref[z, x] = source[x, 1 - high]


def last_kernel(kept_ref, got_ref, out_ref):
    high = lax.div(lax.axis_index("zc"), 2)
    for source, z in ((kept_ref, high), (got_ref, 1 - high)):
        for low in range(2):
            for x in range(2):
                place = lax.rem(2 * z + low + 4 - FIRST_ZC, 4)
                out_ref[2 * place + x] = source[low, x]


def pair_kernel(near_ref, after_ref, out_ref):
    del after_ref
    for h in range(KV_HEADS):
        at = slice(h * HEAD_DIM, (h + 1) * HEAD_DIM)
        first = (h % 2) * 2 * HEAD_DIM
        for i in range(2):
            out_ref[h // 2, :, first + i * HEAD_DIM : first + (i + 1) * HEAD_DIM] = near_ref[i, :, at]


def pack_keys_kernel(axis, pairs_ref, mine_ref, got_ref, out_ref):
    clean = jnp.where(lax.axis_index(axis) == 1, got_ref[...], mine_ref[...])
    for h in range(KV_HEADS):
        first = (h % 2) * 3 * HEAD_DIM
        near = pairs_ref[h // 2, :, (h % 2) * 2 * HEAD_DIM : (h % 2 + 1) * 2 * HEAD_DIM]
        place = (h // 2 + FIRST_ZC) % 4
        for z in (place, place + 4):
            i = Z_ORDER.index(z)
            out_ref[i, :, first : first + 2 * HEAD_DIM] = near
            out_ref[i, :, first + 2 * HEAD_DIM : first + 3 * HEAD_DIM] = clean[:, h * HEAD_DIM : (h + 1) * HEAD_DIM]


def spread_kernel(served_ref, after_ref, out_ref):
    del after_ref
    rows = served_ref.shape[0] * served_ref.shape[1]
    each = 3 * HEAD_DIM
    width = out_ref.shape[2]
    for i in range(out_ref.shape[0]):
        head = (i // 4) % 2
        out_ref[i] = served_ref[:, :, head * each : head * each + width].reshape(rows, width)


def clean_kernel(kv_ref, after_ref, out_ref):
    del after_ref
    out_ref[...] = kv_ref[:, :, 2 * HEAD_DIM :]


def estimate(q_rows, n):
    return pl.CostEstimate(flops=4 * q_rows * n * HEAD_DIM, bytes_accessed=4 * 2**20, transcendentals=q_rows * n)


def call(kernel, out_shape, specs, *operands, cost=None, mib=16):
    outs = (VMEM,) * len(out_shape) if isinstance(out_shape, tuple) else VMEM
    return pl.pallas_call(
        kernel,
        out_shape=out_shape,
        in_specs=specs,
        out_specs=outs,
        cost_estimate=cost,
        compiler_params=pltpu.CompilerParams(vmem_limit_bytes=mib * 2**20),
    )(*operands)


def shaped(*shape, dtype=jnp.bfloat16):
    return jax.ShapeDtypeStruct(shape, dtype)


def shards(query, key, value, clean_key, clean_value, completing, span_mask):
    tok = query.shape[1]
    heads = KV_HEADS
    z_all, served_by, plane_axes = ("zq", "zc"), ("zc", "xb"), ("xa", "xb", "y")
    depth, plane = 8, 16
    anywhere = pl.BlockSpec(memory_space=pl.ANY)

    width = heads * HEAD_DIM
    finished = completing.reshape(1, 1)
    core = lax.axis_index("core")

    def packed(axis, near, mine, got):
        near = call(pair_kernel, shaped(heads // 2, tok, 4 * HEAD_DIM), [VMEM, anywhere], near, mine)
        return call(
            functools.partial(pack_keys_kernel, axis), shaped(depth, tok, 6 * HEAD_DIM), [VMEM] * 3, near, mine, got
        )

    def handed_over(at, key, value, clean_key, clean_value):
        kept, given = (clean_key[0], clean_value[0]) if at == 0 else (clean_value[0], clean_key[0])
        swapped = lax.ppermute(given, ("half", "core"), [(at, 1 - at)])
        picked = jnp.where(core == at, kept, swapped)
        handed = lax.ppermute(
            picked, ("half",) + z_all, [(z, depth + (z + depth // 2) % depth) for z in range(depth)]
        )
        near = jnp.stack([jnp.where(picked != picked, picked, a[0]) for a in (key, value)])
        return packed("half", near, picked, handed)

    def swapped_only(key, value, clean_key, clean_value):
        mine = jnp.where(core == 0, clean_key[0], clean_value[0])
        got = lax.ppermute(clean_value[0], ("half", "core"), [(2, 3)])
        return packed("core", jnp.stack([key[0], value[0]]), mine, got)

    branches = (functools.partial(handed_over, 0), functools.partial(handed_over, 1), swapped_only)
    kv = lax.switch(completing[0], branches, key, value, clean_key, clean_value)
    part = heads // 2
    keep, send = pl.pallas_call(
        stage_kernel,
        out_shape=(shaped(part, tok, WIDE),) * 2,
        in_specs=[anywhere] * 2,
        out_specs=(VMEM,) * 2,
        scratch_shapes=[pltpu.SemaphoreType.DMA((heads,))],
        compiler_params=pltpu.CompilerParams(vmem_limit_bytes=16 * 2**20),
    )(query, kv)
    got = lax.ppermute(send, "xb", [(0, 1), (1, 0)])
    halves = (shaped(2, 2, tok, WIDE),) * 2
    keep, send = call(second_kernel, halves, [VMEM] * 2, keep, got)
    kv = lax.all_to_all(kv, z_all, 0, 0, axis_index_groups=[Z_ORDER], tiled=True)
    rows, n = heads * tok * GROUP, plane * depth * tok

    def gather(kv, keep, send, width):
        own = call(spread_kernel, shaped(plane, depth * tok, width), [VMEM, anywhere], kv, keep)
        own = lax.all_to_all(own, plane_axes, 0, 0, tiled=True)
        got = lax.ppermute(send, "zc", [(z, z ^ 1) for z in range(4)])
        keep, send = call(third_kernel, halves, [VMEM] * 2, keep, got)
        got = lax.ppermute(send, "zc", [(z, z ^ 2) for z in range(4)])
        return own, call(last_kernel, shaped(heads, tok, WIDE), [VMEM] * 2, keep, got)

    def with_clean(kv, keep, send, finished, span_mask):
        kv, served = gather(kv, keep, send, 3 * HEAD_DIM)
        clean = call(clean_kernel, shaped(plane, depth * tok, HEAD_DIM), [VMEM, anywhere], kv, served)
        other = lax.ppermute(clean, "core", [(0, 1), (1, 0)])
        sums, largest = call(
            functools.partial(own_kernel, 3),
            (shaped(rows, 2 * HEAD_DIM, dtype=jnp.float32), shaped(rows, HEAD_DIM, dtype=jnp.float32)),
            [VMEM] * 2,
            served,
            kv,
            cost=estimate(rows, n),
            mib=40,
        )
        return call(
            functools.partial(far_kernel, 3),
            shaped(heads, tok, WIDE),
            [VMEM] * 7,
            finished,
            span_mask,
            served,
            kv,
            other,
            sums,
            largest,
            cost=estimate(rows, n),
            mib=40,
        )

    def without(kv, keep, send, finished, span_mask):
        kv, served = gather(kv, keep, send, 2 * HEAD_DIM)
        return call(
            functools.partial(alone_kernel, 3),
            shaped(heads, tok, WIDE),
            [VMEM] * 2,
            served,
            kv,
            cost=estimate(rows, n),
            mib=40,
        )

    may_see = 2 * lax.axis_index("half") + 1 > completing[0]
    out = lax.cond(may_see, with_clean, without, kv, keep, send, finished, span_mask)
    out = lax.all_to_all(out, served_by, 0, 0, axis_index_groups=[SERVE_ORDER], tiled=True)
    return jnp.transpose(out, (1, 0, 2)).reshape(1, tok, HEADS * HEAD_DIM)


def solution(mesh):
    grid = Mesh(mesh.devices.reshape(2, 2, 2, 4, 2, 2, 4), ("half", "core", "zq", "zc", "xa", "xb", "y"))
    rows = P(("half", "core"), ("zq", "zc", "xa", "xb", "y"), None)
    return jax.shard_map(
        shards, mesh=grid, in_specs=(rows,) * 5 + (P(), P()), out_specs=rows, check_vma=False
    )
```

```python
import functools
import math

import jax
import jax.numpy as jnp
from jax import lax
from jax.experimental import pallas as pl
from jax.experimental.pallas import tpu as pltpu
from jax.sharding import Mesh
from jax.sharding import PartitionSpec as P

HEAD_DIM = 128
HEADS = 48
KV_HEADS = 8
GROUP = HEADS // KV_HEADS
WIDE = GROUP * HEAD_DIM
BASE = HEAD_DIM**-0.5 * math.log2(math.e)
Z_ORDER = [3, 4, 5, 6, 7, 0, 1, 2]
FIRST_ZC = 1
SERVE_ORDER = [(i + 2 * FIRST_ZC) % 8 for i in range(8)]
VMEM = pl.BlockSpec(memory_space=pltpu.VMEM)


def head_rows(q_ref, first, count):
    rows = q_ref.shape[0] * q_ref.shape[1]
    return jnp.concatenate(
        [
            q_ref[:, :, g * HEAD_DIM : (g + 1) * HEAD_DIM].reshape(rows, HEAD_DIM)
            for g in range(first, first + count)
        ],
        0,
    )


def scores_of(q, k):
    return lax.dot_general(q, k, (((1,), (1,)), ((), ())), preferred_element_type=jnp.float32)


def weigh(scores, v_ones):
    largest = jnp.max(scores, axis=-1, keepdims=True)
    weights = jnp.exp2((scores - largest) * BASE).astype(jnp.bfloat16)
    return largest, jnp.dot(weights, v_ones, preferred_element_type=jnp.float32)


def with_ones(v):
    return jnp.concatenate([v, jnp.ones_like(v)], 1)


def own_kernel(count, q_ref, kv_ref, sums_ref, largest_ref):
    n = kv_ref.shape[0] * kv_ref.shape[1]
    rows = q_ref.shape[0] * q_ref.shape[1]
    k = kv_ref[:, :, :HEAD_DIM].reshape(n, HEAD_DIM)
    v_ones = with_ones(kv_ref[:, :, HEAD_DIM : 2 * HEAD_DIM].reshape(n, HEAD_DIM))
    firsts = range(0, GROUP, count)
    scores = [scores_of(head_rows(q_ref, first, count), k) for first in firsts]
    for first, block in zip(firsts, scores):
        at = slice(first * rows, (first + count) * rows)
        largest, sums = weigh(block, v_ones)
        sums_ref[at, :] = sums
        largest_ref[at, :] = jnp.broadcast_to(largest, (count * rows, HEAD_DIM))


def alone_kernel(count, q_ref, kv_ref, out_ref):
    n = kv_ref.shape[0] * kv_ref.shape[1]
    blocks, rows_each = q_ref.shape[0], q_ref.shape[1]
    rows = blocks * rows_each
    k = kv_ref[:, :, :HEAD_DIM].reshape(n, HEAD_DIM)
    v_ones = with_ones(kv_ref[:, :, HEAD_DIM : 2 * HEAD_DIM].reshape(n, HEAD_DIM))
    firsts = range(0, GROUP, count)
    scores = [scores_of(head_rows(q_ref, first, count), k) for first in firsts]
    for first, block in zip(firsts, scores):
        largest, sums = weigh(block, v_ones)
        out = sums[:, :HEAD_DIM] / sums[:, HEAD_DIM:]
        for i in range(count):
            g = first + i
            out_ref[:, :, g * HEAD_DIM : (g + 1) * HEAD_DIM] = (
                out[i * rows : (i + 1) * rows].astype(out_ref.dtype).reshape(blocks, rows_each, HEAD_DIM)
            )


def far_kernel(count, seen_ref, q_ref, kv_ref, other_ref, sums_ref, largest_ref, out_ref):
    n = kv_ref.shape[0] * kv_ref.shape[1]
    blocks, rows_each = q_ref.shape[0], q_ref.shape[1]
    rows = blocks * rows_each
    core = lax.axis_index("core")
    seen = jnp.max(seen_ref[...]) > 0.5

    def store(first, total):
        out = total[:, :HEAD_DIM] / total[:, HEAD_DIM:]
        for i in range(count):
            g = first + i
            out_ref[:, :, g * HEAD_DIM : (g + 1) * HEAD_DIM] = (
                out[i * rows : (i + 1) * rows].astype(out_ref.dtype).reshape(blocks, rows_each, HEAD_DIM)
            )

    @pl.when(seen)
    def _():
        mine = kv_ref[:, :, 2 * HEAD_DIM :].reshape(n, HEAD_DIM)
        other = other_ref[...].reshape(n, HEAD_DIM)
        keys_here = core == 0
        k = jnp.where(keys_here, mine, other)
        v_ones = with_ones(jnp.where(keys_here, other, mine))
        firsts = range(0, GROUP, count)
        scores = [scores_of(head_rows(q_ref, first, count), k) for first in firsts]
        for first, block in zip(firsts, scores):
            at = slice(first * rows, (first + count) * rows)
            largest, sums = weigh(block, v_ones)
            before = largest_ref[at, :]
            after = jnp.maximum(before, largest)
            old = jnp.exp2((before - after) * BASE)
            new = jnp.exp2((largest - after) * BASE)
            old, new = jnp.concatenate([old, old], 1), jnp.concatenate([new, new], 1)
            store(first, sums_ref[at, :] * old + sums * new)

    @pl.when(jnp.logical_not(seen))
    def _():
        for first in range(0, GROUP, count):
            store(first, sums_ref[first * rows : (first + count) * rows, :])


def stage_kernel(query_ref, after_ref, keep_ref, send_ref, sems):
    del after_ref
    xb = lax.axis_index("xb")
    copies = []
    for z in range(KV_HEADS // 2):
        for i, (target, x) in enumerate(((keep_ref, xb), (send_ref, 1 - xb))):
            head = (z - FIRST_ZC) % 4 * 2 + x
            at = pl.ds(pl.multiple_of(head * WIDE, WIDE), WIDE)
            copies.append(pltpu.make_async_copy(query_ref.at[0, :, at], target.at[z], sems.at[2 * z + i]))
    for copy in copies:
        copy.start()
    for copy in copies:
        copy.wait()


def second_kernel(kept_ref, got_ref, keep_ref, send_ref):
    xb, low = lax.axis_index("xb"), lax.rem(lax.axis_index("zc"), 2)
    for source, x in ((kept_ref, xb), (got_ref, 1 - xb)):
        for high in range(2):
            keep_ref[x, high] = source[2 * high + low]
            send_ref[x, high] = source[2 * high + 1 - low]


def third_kernel(completing_ref, mask_ref, kept_ref, got_ref, keep_ref, send_ref, seen_ref):
    section = lax.axis_index("half") * 2 + lax.axis_index("core")
    finished = jnp.broadcast_to(completing_ref[...], mask_ref.shape)
    at_row = lax.broadcasted_iota(jnp.int32, mask_ref.shape, 0) == section
    at_column = lax.broadcasted_iota(jnp.int32, mask_ref.shape, 1) == finished
    visible = jnp.logical_and(mask_ref[...] == 1, section > finished)
    hit = jnp.logical_and(jnp.logical_and(at_row, at_column), visible)
    seen_ref[...] = jnp.broadcast_to(jnp.max(jnp.where(hit, 1.0, 0.0), keepdims=True), seen_ref.shape)
    zc = lax.axis_index("zc")
    low, high = lax.rem(zc, 2), lax.div(zc, 2)
    for source, z in ((kept_ref, low), (got_ref, 1 - low)):
        for x in range(2):
            keep_ref[z, x] = source[x, high]
            send_ref[z, x] = source[x, 1 - high]


def last_kernel(kept_ref, got_ref, out_ref):
    high = lax.div(lax.axis_index("zc"), 2)
    for source, z in ((kept_ref, high), (got_ref, 1 - high)):
        for low in range(2):
            for x in range(2):
                place = lax.rem(2 * z + low + 4 - FIRST_ZC, 4)
                out_ref[2 * place + x] = source[low, x]


def pair_kernel(near_ref, after_ref, out_ref):
    del after_ref
    for h in range(KV_HEADS):
        at = slice(h * HEAD_DIM, (h + 1) * HEAD_DIM)
        first = (h % 2) * 2 * HEAD_DIM
        for i in range(2):
            out_ref[h // 2, :, first + i * HEAD_DIM : first + (i + 1) * HEAD_DIM] = near_ref[i, :, at]


def pack_keys_kernel(axis, pairs_ref, mine_ref, got_ref, out_ref):
    clean = jnp.where(lax.axis_index(axis) == 1, got_ref[...], mine_ref[...])
    for h in range(KV_HEADS):
        first = (h % 2) * 3 * HEAD_DIM
        near = pairs_ref[h // 2, :, (h % 2) * 2 * HEAD_DIM : (h % 2 + 1) * 2 * HEAD_DIM]
        place = (h // 2 + FIRST_ZC) % 4
        for z in (place, place + 4):
            i = Z_ORDER.index(z)
            out_ref[i, :, first : first + 2 * HEAD_DIM] = near
            out_ref[i, :, first + 2 * HEAD_DIM : first + 3 * HEAD_DIM] = clean[:, h * HEAD_DIM : (h + 1) * HEAD_DIM]


def spread_kernel(served_ref, after_ref, out_ref):
    del after_ref
    rows = served_ref.shape[0] * served_ref.shape[1]
    each = 3 * HEAD_DIM
    width = out_ref.shape[2]
    for i in range(out_ref.shape[0]):
        head = (i // 4) % 2
        out_ref[i] = served_ref[:, :, head * each : head * each + width].reshape(rows, width)


def clean_kernel(kv_ref, after_ref, out_ref):
    del after_ref
    out_ref[...] = kv_ref[:, :, 2 * HEAD_DIM :]


def estimate(q_rows, n):
    return pl.CostEstimate(flops=4 * q_rows * n * HEAD_DIM, bytes_accessed=4 * 2**20, transcendentals=q_rows * n)


def call(kernel, out_shape, specs, *operands, cost=None, mib=16):
    outs = (VMEM,) * len(out_shape) if isinstance(out_shape, tuple) else VMEM
    return pl.pallas_call(
        kernel,
        out_shape=out_shape,
        in_specs=specs,
        out_specs=outs,
        cost_estimate=cost,
        compiler_params=pltpu.CompilerParams(vmem_limit_bytes=mib * 2**20),
    )(*operands)


def shaped(*shape, dtype=jnp.bfloat16):
    return jax.ShapeDtypeStruct(shape, dtype)


def shards(query, key, value, clean_key, clean_value, completing, span_mask):
    tok = query.shape[1]
    heads = KV_HEADS
    z_all, served_by, plane_axes = ("zq", "zc"), ("zc", "xb"), ("xa", "xb", "y")
    depth, plane = 8, 16
    anywhere = pl.BlockSpec(memory_space=pl.ANY)

    width = heads * HEAD_DIM
    finished = completing.reshape(1, 1)
    core = lax.axis_index("core")

    def packed(axis, near, mine, got):
        near = call(pair_kernel, shaped(heads // 2, tok, 4 * HEAD_DIM), [VMEM, anywhere], near, mine)
        return call(
            functools.partial(pack_keys_kernel, axis), shaped(depth, tok, 6 * HEAD_DIM), [VMEM] * 3, near, mine, got
        )

    def handed_over(at, key, value, clean_key, clean_value):
        kept, given = (clean_key[0], clean_value[0]) if at == 0 else (clean_value[0], clean_key[0])
        swapped = lax.ppermute(given, ("half", "core"), [(at, 1 - at)])
        picked = jnp.where(core == at, kept, swapped)
        handed = lax.ppermute(
            picked, ("half",) + z_all, [(z, depth + (z + depth // 2) % depth) for z in range(depth)]
        )
        near = jnp.stack([jnp.where(picked != picked, picked, a[0]) for a in (key, value)])
        return packed("half", near, picked, handed)

    def swapped_only(key, value, clean_key, clean_value):
        mine = jnp.where(core == 0, clean_key[0], clean_value[0])
        got = lax.ppermute(clean_value[0], ("half", "core"), [(2, 3)])
        return packed("core", jnp.stack([key[0], value[0]]), mine, got)

    branches = (functools.partial(handed_over, 0), functools.partial(handed_over, 1), swapped_only)
    kv = lax.switch(completing[0], branches, key, value, clean_key, clean_value)
    part = heads // 2
    keep, send = pl.pallas_call(
        stage_kernel,
        out_shape=(shaped(part, tok, WIDE),) * 2,
        in_specs=[anywhere] * 2,
        out_specs=(VMEM,) * 2,
        scratch_shapes=[pltpu.SemaphoreType.DMA((heads,))],
        compiler_params=pltpu.CompilerParams(vmem_limit_bytes=16 * 2**20),
    )(query, kv)
    got = lax.ppermute(send, "xb", [(0, 1), (1, 0)])
    halves = (shaped(2, 2, tok, WIDE),) * 2
    keep, send = call(second_kernel, halves, [VMEM] * 2, keep, got)
    kv = lax.all_to_all(kv, z_all, 0, 0, axis_index_groups=[Z_ORDER], tiled=True)
    rows, n = heads * tok * GROUP, plane * depth * tok

    def gather(kv, keep, send, finished, span_mask, width):
        own = call(spread_kernel, shaped(plane, depth * tok, width), [VMEM, anywhere], kv, keep)
        own = lax.all_to_all(own, plane_axes, 0, 0, tiled=True)
        got = lax.ppermute(send, "zc", [(z, z ^ 1) for z in range(4)])
        outs = halves + (shaped(8, HEAD_DIM, dtype=jnp.float32),)
        keep, send, seen = call(third_kernel, outs, [VMEM] * 4, finished, span_mask, keep, got)
        got = lax.ppermute(send, "zc", [(z, z ^ 2) for z in range(4)])
        return own, call(last_kernel, shaped(heads, tok, WIDE), [VMEM] * 2, keep, got), seen

    def with_clean(kv, keep, send, finished, span_mask):
        kv, served, seen = gather(kv, keep, send, finished, span_mask, 3 * HEAD_DIM)
        clean = call(clean_kernel, shaped(plane, depth * tok, HEAD_DIM), [VMEM, anywhere], kv, served)
        other = lax.ppermute(clean, "core", [(0, 1), (1, 0)])
        sums, largest = call(
            functools.partial(own_kernel, 3),
            (shaped(rows, 2 * HEAD_DIM, dtype=jnp.float32), shaped(rows, HEAD_DIM, dtype=jnp.float32)),
            [VMEM] * 2,
            served,
            kv,
            cost=estimate(rows, n),
            mib=40,
        )
        return call(
            functools.partial(far_kernel, 3),
            shaped(heads, tok, WIDE),
            [VMEM] * 6,
            seen,
            served,
            kv,
            other,
            sums,
            largest,
            cost=estimate(rows, n),
            mib=40,
        )

    def without(kv, keep, send, finished, span_mask):
        kv, served, _ = gather(kv, keep, send, finished, span_mask, 2 * HEAD_DIM)
        return call(
            functools.partial(alone_kernel, 3),
            shaped(heads, tok, WIDE),
            [VMEM] * 2,
            served,
            kv,
            cost=estimate(rows, n),
            mib=40,
        )

    may_see = 2 * lax.axis_index("half") + 1 > completing[0]
    out = lax.cond(may_see, with_clean, without, kv, keep, send, finished, span_mask)
    out = lax.all_to_all(out, served_by, 0, 0, axis_index_groups=[SERVE_ORDER], tiled=True)
    return jnp.transpose(out, (1, 0, 2)).reshape(1, tok, HEADS * HEAD_DIM)


def solution(mesh):
    grid = Mesh(mesh.devices.reshape(2, 2, 2, 4, 2, 2, 4), ("half", "core", "zq", "zc", "xa", "xb", "y"))
    rows = P(("half", "core"), ("zq", "zc", "xa", "xb", "y"), None)
    return jax.shard_map(
        shards, mesh=grid, in_specs=(rows,) * 5 + (P(), P()), out_specs=rows, check_vma=False
    )
```
